512 devices in a mesh: tr: 16 (over z, core), tc: 32 (over x, y).
Axes of the slice: x: 4, y: 8, z: 8, core: 2. Of those that a mesh axis runs over, the one named last changes fastest.
Arguments:
- cov_tiles: float32 [16384, 16384], P('tr', 'tc'), may hold values from -3 to 9, as said below
- block_order: int32 [32], replicated, may hold values from 0 to 31, as said below
- stations: int32 [1, 256], P(None, 'tc'), may hold values from 0 to 31
- obs_values: float32 [1, 256, 512], P(None, 'tc'), may hold values from -0.25 to 0.25
- obs_error: float32 [1, 256], P(None, 'tc'), may hold values from 0.5 to 4
Outputs:
- cov_updated: float32 [16384, 16384], P('tr', 'tc')
The draws below stay inside these ranges and needn't reach their ends.
Inputs may be any that keep to these rules, and one draw needn't show every extreme that they name: `block_order`: a permutation of 0 to 31. `cov_tiles`: the matrix that the live tiles describe, completed by symmetry, is positive definite with diagonal tiles symmetric; tiles that are not live are zero.
All inputs are finite; a program needn't handle non-finite values.
Results may differ from the reference program's by a relative error of at most 0.0001.
Values sent between devices are 32-bit elements; how exact they have to be, the bound alone decides.
No kernel may reach another device: no remote copies, remote signals or barrier semaphores. Data moves between devices by JAX's collectives and lax.ppermute only.
A program may use at most 64 MiB of HBM per device.

```python
import math
import jax
import jax.numpy as jnp
from jax import lax

ORDER = 16384
TILE = 512
NOBS = 256
BATCHES = 1
BLOCKS = 32


def order_from(key):
    return jax.random.permutation(jax.random.fold_in(key, 17), ORDER // TILE).astype(jnp.int32)


def draw_block_order(key, part):
    return order_from(key)


def draw_cov_tiles(key, part):
    count_blocks = ORDER // TILE
    permuted = order_from(key)
    first_key, second_key, third_key = jax.random.split(jax.random.fold_in(key, 29), 3)
    noise = jax.random.normal(first_key, (ORDER, ORDER), jnp.float32)
    loading = jax.random.normal(second_key, (ORDER, 32), jnp.float32)
    spread = jnp.exp(jax.random.uniform(third_key, (ORDER,), jnp.float32, math.log(2.0), math.log(6.0)))
    loading = loading * 0.125
    matrix = (noise + noise.T) * (0.55 / math.sqrt(ORDER)) + jnp.diag(spread)
    matrix = matrix + jnp.dot(loading, loading.T, precision=lax.Precision.HIGHEST, preferred_element_type=jnp.float32)
    positions = jnp.arange(count_blocks, dtype=jnp.int32)
    live = (permuted[:, None] > permuted[None, :]).astype(jnp.float32) + (positions[:, None] == positions[None, :]).astype(jnp.float32)
    spread_mask = jnp.broadcast_to(live[:, None, :, None], (count_blocks, TILE, count_blocks, TILE)).reshape(ORDER, ORDER)
    return matrix * spread_mask


def touch_ends(array, rng, least, high):
    index_at = [jax.random.randint(jax.random.fold_in(rng, axis), (), 0, length) for axis, length in enumerate(array.shape)]
    widest = array.shape.index(max(array.shape))
    beside = index_at[:widest] + [(index_at[widest] + 1) % array.shape[widest]] + index_at[widest + 1:]
    return array.at[tuple(index_at)].set(least).at[tuple(beside)].set(high)


def steps_of(rng, extent, shards, least, top_value):
    def one(axis_at, blocks):
        steps = jax.random.uniform(jax.random.fold_in(jax.random.fold_in(rng, 6), axis_at), (blocks,), jnp.float32, least / len(shards), top_value / len(shards))
        return jnp.repeat(jnp.exp(steps), extent[axis_at] // blocks).reshape((-1,) + (1,) * (len(extent) - axis_at - 1))

    level = one(*shards[0])
    for cut in shards[1:]:
        level = level * one(*cut)
    return level


def scatter_about(stream_key, extent, width, limit, shards=(), kind=jnp.bfloat16):
    factor_of = steps_of(stream_key, extent, shards, -0.22, 0.18) if shards else 1.0
    array = jax.random.normal(stream_key, extent, jnp.float32) * width * factor_of
    return jnp.minimum(jnp.maximum(array, -limit), limit).astype(kind)


def setup_inputs(seed: int = 0) -> dict:
    key_list = jax.random.split(jax.random.key(seed), 6)
    cov_tiles = draw_cov_tiles(jax.random.fold_in(key_list[5], 71), 0)
    block_order = draw_block_order(jax.random.fold_in(key_list[5], 71), 0)
    stations = touch_ends(jax.random.randint(key_list[2], (BATCHES, NOBS), 0, BLOCKS), jax.random.fold_in(key_list[2], 1), 0, BLOCKS - 1).astype(jnp.int32)
    obs_values = scatter_about(key_list[3], (BATCHES, NOBS, TILE), TILE ** -0.5, 0.25, ((1, 32),), jnp.float32)
    obs_error = jnp.clip(jnp.exp(math.log(4.0) - 2.0794415 * jax.random.uniform(key_list[4], (BATCHES, NOBS), jnp.float32) ** steps_of(key_list[4], (BATCHES, NOBS), ((1, 32),), -0.2, 0.2)), 0.5, 4.0)
    return dict(cov_tiles=cov_tiles, block_order=block_order, stations=stations, obs_values=obs_values, obs_error=obs_error)


precise = lax.Precision.HIGHEST

def tile_spread(blockwise):
    return jnp.broadcast_to(blockwise[:, None, :, None], (BLOCKS, TILE, BLOCKS, TILE)).reshape(ORDER, ORDER)

def reference(cov_tiles, block_order, stations, obs_values, obs_error):
    positions = jnp.arange(BLOCKS, dtype=jnp.int32)
    below_mask = (block_order[:, None] > block_order[None, :]).astype(jnp.float32)
    on_diagonal = (positions[:, None] == positions[None, :]).astype(jnp.float32)
    strict = cov_tiles * tile_spread(below_mask)
    covariance = strict + strict.T + cov_tiles * tile_spread(on_diagonal)
    for batch_index in range(BATCHES):
        select = (stations[batch_index][None, :] == block_order[:, None]).astype(jnp.float32)
        design = (select[:, None, :] * obs_values[batch_index].T[None, :, :]).reshape(ORDER, NOBS)
        cross_cov = jnp.dot(covariance.astype(jnp.float32), design.astype(jnp.float32), precision=precise, preferred_element_type=jnp.float32)
        innovation = jnp.dot(design.T.astype(jnp.float32), cross_cov.astype(jnp.float32), precision=precise, preferred_element_type=jnp.float32)
        innovation = innovation + jnp.diag(obs_error[batch_index])
        factor = jnp.linalg.cholesky(innovation)
        scaled = lax.linalg.triangular_solve(factor, cross_cov, left_side=False, lower=True, transpose_a=True)
        covariance = covariance - jnp.dot(scaled.astype(jnp.float32), scaled.T.astype(jnp.float32), precision=precise, preferred_element_type=jnp.float32)
    return covariance * tile_spread(below_mask + on_diagonal)
```

```python
import jax
import jax.numpy as jnp
from jax import lax
from jax.sharding import Mesh
from jax.sharding import PartitionSpec as P

TR = ("z", "k")
TC = ("x", "yh", "yl")
NEAR = ("z", "k", "yl")
ALL = ("z", "k", "x", "yh", "yl")
SLOTS = 32
PAIR_SLOTS = 48
LANES = 128

precise = lax.Precision.HIGHEST


def dot(former, latter, dims=((1,), (0,))):
    return lax.dot_general(
        former, latter, (dims, ((), ())), precision=precise, preferred_element_type=jnp.float32
    )


def exchange(array, axes):
    return lax.all_to_all(array, axes, 0, 0, tiled=True)


def spread(array, axes):
    count = lax.axis_size(axes)
    return exchange(jnp.broadcast_to(array[None], (count, *array.shape)), axes)


def body(cov, order, stations, obs_values, obs_error):
    rows, tile = cov.shape
    nobs_own = obs_values.shape[1]
    tr_size, tc_size = lax.axis_size(TR), lax.axis_size(TC)
    nobs = nobs_own * tc_size
    share = tile // tc_size
    halves = share // 8
    row = lax.axis_index(TR)
    col = lax.axis_index(TC)
    blocks = order.shape[0]

    tail = jnp.stack([stations[0].astype(jnp.float32), obs_error[0]], axis=1)
    packed = jnp.concatenate(
        [obs_values[0], jnp.pad(tail, ((0, 0), (0, LANES - tail.shape[1])))], axis=1
    )
    everything = spread(packed, TC).reshape(nobs, tile + LANES)
    values = everything[:, :tile]
    station = everything[:, tile].astype(jnp.int32)
    errors = everything[:, tile + 1]

    numbers = jnp.arange(nobs, dtype=jnp.int32)
    position = jnp.sum(
        jnp.where(station[None, :] == order[:, None], jnp.arange(blocks, dtype=jnp.int32)[:, None], 0), axis=0
    )
    before = numbers[:, None] < numbers[None, :]
    rank = jnp.sum(((station[:, None] == station[None, :]) & before).astype(jnp.int32), axis=0)
    pair = position // 2
    pair_rank = jnp.sum(((pair[:, None] == pair[None, :]) & before).astype(jnp.int32), axis=0)
    rounds = 1 + jnp.maximum(jnp.max(rank) // SLOTS, jnp.max(pair_rank) // PAIR_SLOTS)

    lane = jnp.arange(LANES, dtype=jnp.int32)
    weighted = [values * (position == 2 * row + t).astype(jnp.float32)[:, None] for t in range(2)]

    def one_round(number, carry):
        cross_rows, gram_rows = carry
        slot = rank - number * SLOTS
        code = jnp.where((slot >= 0) & (slot < SLOTS), position * SLOTS + slot, -1)
        pair_slot = pair_rank - number * PAIR_SLOTS
        pair_code = jnp.where(
            (pair_slot >= 0) & (pair_slot < PAIR_SLOTS), pair * PAIR_SLOTS + pair_slot, -1
        )
        pick = (code[None, :] == (col * SLOTS + lane % SLOTS)[:, None]).astype(jnp.float32)
        column_weights = dot(pick, values)
        row_terms = dot(cov, column_weights, ((1,), (1,)))
        pair_pick = (pair_code[None, :] == (row * PAIR_SLOTS + lane % PAIR_SLOTS)[:, None]) & (
            lane < 2 * PAIR_SLOTS
        )[:, None]
        pair_weights = []
        for t in range(2):
            off_diagonal = (2 * row + t) != col
            chosen = pair_pick & (position == 2 * row + t)[None, :] & off_diagonal
            pair_weights.append(dot(chosen.astype(jnp.float32), values))
        column_terms = dot(cov[:tile], pair_weights[0], ((0,), (1,))) + dot(
            cov[tile:], pair_weights[1], ((0,), (1,))
        )
        gram_terms = dot(weighted[0], row_terms[:tile]) + dot(weighted[1], row_terms[tile:])
        shaped = row_terms.reshape(2, tc_size, halves, 8, LANES)
        first = sum(
            jnp.where(lane // SLOTS == t * halves + m, shaped[t, :, m], 0.0)
            for t in range(2)
            for m in range(halves)
        )
        shaped = column_terms.reshape(tc_size, halves, 8, LANES)
        second = sum(
            jnp.where(lane // PAIR_SLOTS == m, shaped[:, m], 0.0) for m in range(halves)
        )
        second = jnp.where(lane >= LANES - SLOTS, gram_terms.reshape(tc_size, 8, LANES), second)
        arrived = exchange(jnp.concatenate([first, second], axis=1), TC)

        slots = jnp.arange(tc_size * SLOTS, dtype=jnp.int32)
        place = (slots[:, None] == code[None, :]).astype(jnp.float32)
        first = arrived[:, :8].reshape(tc_size, 8, 2 * halves, SLOTS)
        first = first.transpose(2, 1, 0, 3).reshape(2 * share, tc_size * SLOTS)
        gram = arrived[:, 8:, LANES - SLOTS :].transpose(1, 0, 2).reshape(8, tc_size * SLOTS)
        placed = dot(jnp.concatenate([first, gram]), place)
        gram = placed[2 * share :].reshape(8, nobs // LANES, LANES).transpose(1, 0, 2)
        second = jnp.concatenate(
            [
                arrived[:, 8:].reshape(tr_size, 2, 8, LANES),
                jnp.broadcast_to(gram[None], (tr_size, *gram.shape)),
            ],
            axis=1,
        )
        arrived = exchange(second, TR)
        pair_slots = jnp.arange(tr_size * PAIR_SLOTS, dtype=jnp.int32)
        pair_place = (pair_slots[:, None] == pair_code[None, :]).astype(jnp.float32)
        second = arrived[:, :2, :, : halves * PAIR_SLOTS].reshape(tr_size, 2, 8, halves, PAIR_SLOTS)
        second = second.transpose(1, 3, 2, 0, 4).reshape(2 * share, tr_size * PAIR_SLOTS)
        gram = jnp.sum(arrived[:, 2:], axis=0).transpose(1, 0, 2).reshape(8, nobs)
        cross_rows = cross_rows + placed[: 2 * share] + dot(second, pair_place)
        return cross_rows, gram_rows + gram

    cross_rows, gram_rows = lax.fori_loop(
        0,
        rounds,
        one_round,
        (jnp.zeros((2 * share, nobs), jnp.float32), jnp.zeros((8, nobs), jnp.float32)),
    )

    moves = [
        (r * tc_size + c, (c // 2) * tc_size + 2 * r + c % 2)
        for r in range(tr_size)
        for c in range(tc_size)
    ]
    moved = lax.ppermute(cross_rows, ALL, moves)
    arrived = spread(jnp.concatenate([cross_rows, gram_rows]), TC)
    row_cross = arrived[:, : 2 * share].reshape(tc_size, 2, share, nobs)
    row_cross = row_cross.transpose(1, 0, 2, 3).reshape(rows, nobs)
    gram = arrived[:, 2 * share :].reshape(nobs, nobs)
    near = jnp.broadcast_to(moved.reshape(1, 2, share, nobs), (tr_size, 2, share, nobs))
    col_cross = exchange(near.reshape(2 * tr_size, share, nobs), NEAR).reshape(tile, nobs)

    both = gram + gram.T
    same = position[:, None] == position[None, :]
    innovation = jnp.where(same, 0.5 * both, both) + jnp.diag(errors)
    factor = jnp.linalg.cholesky(innovation)
    inverse = lax.linalg.triangular_solve(
        factor, jnp.eye(nobs, dtype=jnp.float32), left_side=True, lower=True
    )
    row_scaled = dot(row_cross, inverse, ((1,), (1,)))
    col_scaled = dot(col_cross, inverse, ((1,), (1,)))
    places = 2 * row + jnp.arange(2, dtype=jnp.int32)
    row_order = lax.dynamic_slice_in_dim(order, 2 * row, 2)
    col_order = lax.dynamic_slice_in_dim(order, col, 1)
    keep = ((row_order > col_order) | (places == col)).astype(jnp.float32)
    updated = cov - dot(row_scaled, col_scaled, ((1,), (1,)))
    return (updated.reshape(2, tile, tile) * keep[:, None, None]).reshape(rows, tile)


def solution(mesh):
    tr_size, tc_size = mesh.shape["tr"], mesh.shape["tc"]
    y_size = 8 if tc_size % 8 == 0 else tc_size
    split = Mesh(
        mesh.devices.reshape(tr_size // 2, 2, tc_size // y_size, y_size // 2, 2), ALL
    )
    return jax.shard_map(
        body,
        mesh=split,
        in_specs=(P(TR, TC), P(), P(None, TC), P(None, TC, None), P(None, TC)),
        out_specs=P(TR, TC),
        check_vma=False,
    )
```

```python
import jax
import jax.numpy as jnp
from jax import lax
from jax.experimental import pallas as pl
from jax.experimental.pallas import tpu as pltpu
from jax.sharding import Mesh
from jax.sharding import PartitionSpec as P

TR = ("z", "k")
TC = ("x", "yh", "yl")
NEAR = ("z", "k", "yl")
ALL = ("z", "k", "x", "yh", "yl")
SLOTS = 32
PAIR_SLOTS = 48
LANES = 128
GROUPS = LANES // SLOTS
SETTLED = 1e-7

precise = lax.Precision.HIGHEST


def dot(former, latter, dims=((1,), (0,))):
    return lax.dot_general(
        former, latter, (dims, ((), ())), precision=precise, preferred_element_type=jnp.float32
    )


def iota(shape, dim):
    return lax.broadcasted_iota(jnp.int32, shape, dim)


def exchange(array, axes):
    return lax.all_to_all(array, axes, 0, 0, tiled=True)


def in_vmem(count):
    return [pl.BlockSpec(memory_space=pltpu.VMEM)] * count


def params():
    return pltpu.CompilerParams(vmem_limit_bytes=48 * 1024 * 1024)


def as_row(column):
    return jnp.broadcast_to(column, (column.shape[0], LANES)).T[:1]


def codes_kernel(everything, order_column, codes, rounds):
    nobs = everything.shape[0]
    tile = everything.shape[1] - LANES
    station = everything[:, tile : tile + 1].astype(jnp.int32)
    station_row = as_row(everything[:, tile : tile + 1]).astype(jnp.int32)
    blocks = order_column.shape[0]
    position = jnp.sum(
        jnp.where(order_column[...] == station_row, iota((blocks, nobs), 0), 0), axis=0, keepdims=True
    )
    position_column = jnp.broadcast_to(position, (LANES, nobs)).astype(jnp.float32).T[:, :1].astype(jnp.int32)
    before = iota((nobs, nobs), 0) < iota((nobs, nobs), 1)
    rank = jnp.sum(((station == station_row) & before).astype(jnp.int32), axis=0, keepdims=True)
    paired = (position_column >> 1) == (position >> 1)
    pair_rank = jnp.sum((paired & before).astype(jnp.int32), axis=0, keepdims=True)
    codes[0:1] = position
    codes[1:2] = rank
    codes[2:3] = pair_rank
    codes[3:8] = jnp.zeros((5, nobs), jnp.int32)
    rounds[0] = 1 + jnp.maximum(jnp.max(rank) // SLOTS, jnp.max(pair_rank) // PAIR_SLOTS)


def make_codes(everything, order):
    return pl.pallas_call(
        codes_kernel,
        out_shape=(
            jax.ShapeDtypeStruct((8, everything.shape[0]), jnp.int32),
            jax.ShapeDtypeStruct((1,), jnp.int32),
        ),
        in_specs=in_vmem(2),
        out_specs=(pl.BlockSpec(memory_space=pltpu.VMEM), pl.BlockSpec(memory_space=pltpu.SMEM)),
        compiler_params=params(),
    )(everything, order.reshape(-1, 1))


def slot_codes(codes, number):
    position = codes[0:1]
    slot = codes[1:2] - number * SLOTS
    code = jnp.where((slot >= 0) & (slot < SLOTS), position * SLOTS + slot, -1)
    pair_slot = codes[2:3] - number * PAIR_SLOTS
    pair_code = jnp.where(
        (pair_slot >= 0) & (pair_slot < PAIR_SLOTS), (position >> 1) * PAIR_SLOTS + pair_slot, -1
    )
    return position, code, pair_code


def terms_kernel(where, everything, codes, cov, out):
    row, col, number = where[0], where[1], where[2]
    rows, tile = cov.shape
    nobs = everything.shape[0]
    groups = out.shape[0]
    halves = tile // groups // 8
    values = everything[:, :tile]
    position, code, pair_code = slot_codes(codes, number)
    sub = iota((LANES, nobs), 0)
    pick = (code == col * SLOTS + sub % SLOTS).astype(jnp.float32)
    column_weights = dot(pick, values)
    row_terms = dot(cov[...], column_weights, ((1,), (1,)))
    pair_pick = (pair_code == row * PAIR_SLOTS + sub % PAIR_SLOTS) & (sub < 2 * PAIR_SLOTS)
    column_terms = jnp.zeros((LANES, tile), jnp.float32)
    gram_terms = jnp.zeros((nobs, LANES), jnp.float32)
    position_column = jnp.broadcast_to(position, (LANES, nobs)).astype(jnp.float32).T[:, :1]
    for t in range(2):
        place = 2 * row + t
        off_diagonal = jnp.where(place != col, 1.0, 0.0)
        chosen = (pair_pick & (position == place)).astype(jnp.float32) * off_diagonal
        column_terms += dot(dot(chosen, values), cov[t * tile : (t + 1) * tile])
        weighted = values * (position_column == place.astype(jnp.float32)).astype(jnp.float32)
        gram_terms += dot(weighted, row_terms[t * tile : (t + 1) * tile])
    lane = iota((groups, 8, LANES), 2)
    shaped = row_terms.reshape(2, groups, halves, 8, LANES)
    first = jnp.zeros((groups, 8, LANES), jnp.float32)
    for t in range(2):
        for m in range(halves):
            first = jnp.where(lane // SLOTS == t * halves + m, shaped[t, :, m], first)
    out[:, :8] = first
    shaped = column_terms.T.reshape(groups, halves, 8, LANES)
    second = gram_terms.reshape(groups, 8, LANES)
    for m in range(halves):
        second = jnp.where(lane // PAIR_SLOTS == m, shaped[:, m], second)
    out[:, 8:] = second


def make_terms(where, everything, codes, cov, groups):
    return pl.pallas_call(
        terms_kernel,
        out_shape=jax.ShapeDtypeStruct((groups, 16, LANES), jnp.float32),
        in_specs=[pl.BlockSpec(memory_space=pltpu.SMEM), *in_vmem(3)],
        out_specs=pl.BlockSpec(memory_space=pltpu.VMEM),
        compiler_params=params(),
    )(where, everything, codes, cov)


def place_kernel(where, codes, arrived, placed, second):
    nobs = codes.shape[1]
    groups = arrived.shape[0]
    code = slot_codes(codes, where[2])[1]
    lane = iota((8, LANES), 1)
    parts = GROUPS + 1
    lines = [[] for _ in range(parts)]
    for g in range(groups // GROUPS):
        for part in range(parts):
            line = None
            for q in range(GROUPS):
                at, source = (part, arrived[g * GROUPS + q, :8]) if part < GROUPS else (
                    GROUPS - 1,
                    arrived[g * GROUPS + q, 8:],
                )
                shift = (q - at) * SLOTS % LANES
                turned = pltpu.roll(source, shift, 1) if shift else source
                line = turned if line is None else jnp.where(lane // SLOTS == q, turned, line)
            lines[part].append(line)
    former = jnp.concatenate([jnp.concatenate(line, axis=1) for line in lines], axis=0)
    spots = (iota((groups * SLOTS, nobs), 0) == code).astype(jnp.float32)
    result = dot(former, spots)
    placed[...] = result[: 8 * GROUPS]
    gram = result[8 * GROUPS :]
    for r in range(second.shape[0]):
        for t in range(2):
            second[r, t] = arrived[2 * r + t, 8:]
        for part in range(nobs // LANES):
            second[r, 2 + part] = gram[:, part * LANES : (part + 1) * LANES]


def place_rows(where, codes, arrived, tr_size):
    nobs = codes.shape[1]
    return pl.pallas_call(
        place_kernel,
        out_shape=(
            jax.ShapeDtypeStruct((8 * GROUPS, nobs), jnp.float32),
            jax.ShapeDtypeStruct((tr_size, 2 + nobs // LANES, 8, LANES), jnp.float32),
        ),
        in_specs=[pl.BlockSpec(memory_space=pltpu.SMEM), *in_vmem(2)],
        out_specs=tuple(in_vmem(2)),
        compiler_params=params(),
    )(where, codes, arrived)


def gather_kernel(where, codes, placed, arrived, out):
    nobs = codes.shape[1]
    pair_code = slot_codes(codes, where[2])[2]
    lane = iota((8, LANES), 1)
    pairs = arrived.shape[0]
    halves = GROUPS // 2
    lines = []
    for t in range(2):
        for m in range(halves):
            inside = lane // PAIR_SLOTS == m
            lines.append(
                jnp.concatenate([jnp.where(inside, arrived[r, t], 0.0) for r in range(pairs)], axis=1)
            )
    former = jnp.concatenate(lines, axis=0)
    at = iota((pairs * LANES, nobs), 0)
    within = at % LANES
    spot = jnp.where(within < 2 * PAIR_SLOTS, at // LANES * PAIR_SLOTS + within % PAIR_SLOTS, -2)
    spots = (spot == pair_code).astype(jnp.float32)
    out[: 8 * GROUPS] = placed[...] + dot(former, spots)
    for part in range(nobs // LANES):
        total = arrived[0, 2 + part]
        for r in range(1, pairs):
            total = total + arrived[r, 2 + part]
        out[8 * GROUPS :, part * LANES : (part + 1) * LANES] = total


def gather_rows(where, codes, placed, arrived):
    nobs = codes.shape[1]
    return pl.pallas_call(
        gather_kernel,
        out_shape=jax.ShapeDtypeStruct((8 * GROUPS + 8, nobs), jnp.float32),
        in_specs=[pl.BlockSpec(memory_space=pltpu.SMEM), *in_vmem(3)],
        out_specs=pl.BlockSpec(memory_space=pltpu.VMEM),
        compiler_params=params(),
    )(where, codes, placed, arrived)


def inverse_kernel(everything, codes, arrived, out):
    nobs = codes.shape[1]
    tile = everything.shape[1] - LANES
    gram = arrived[:, 8 * GROUPS :].reshape(nobs, nobs)
    both = gram + gram.T
    position = codes[0:1]
    position_column = jnp.broadcast_to(position, (LANES, nobs)).astype(jnp.float32).T[:, :1].astype(jnp.int32)
    errors = everything[:, tile + 1 : tile + 2]
    unit = (iota((nobs, nobs), 0) == iota((nobs, nobs), 1)).astype(jnp.float32)
    innovation = jnp.where(position == position_column, 0.5 * both, both) + unit * errors
    low = jnp.min(errors, keepdims=True)
    sums = jnp.sum(jnp.abs(innovation), axis=1, keepdims=True)
    high = jnp.maximum(jnp.max(sums, keepdims=True), low)
    ratio = (high - low) / (high + low)
    base = 2.0 / (low + high)
    square = ratio * ratio
    scale = 2.0 / (2.0 - square)
    start = (scale * base) * (2.0 * unit - base * innovation)

    def unsettled(carry):
        count, left, _, _ = carry
        return (left > SETTLED) & (count < 64)

    def step(carry):
        count, _, spread, inverse = carry
        gap = spread * spread
        grow = 2.0 / (2.0 - gap)
        shrunk = gap * 0.5 * grow
        rest = 2.0 * unit - dot(innovation, inverse)
        return count + 1, jnp.max(shrunk), shrunk, grow * dot(inverse, rest)

    first = square * 0.5 * scale
    result = lax.while_loop(unsettled, step, (jnp.int32(0), jnp.max(first), first, start))
    out[...] = result[3]


def invert(everything, codes, arrived):
    nobs = codes.shape[1]
    return pl.pallas_call(
        inverse_kernel,
        out_shape=jax.ShapeDtypeStruct((nobs, nobs), jnp.float32),
        in_specs=in_vmem(3),
        out_specs=pl.BlockSpec(memory_space=pltpu.VMEM),
        compiler_params=params(),
        cost_estimate=pl.CostEstimate(
            flops=150 * nobs**3, bytes_accessed=8 * nobs * nobs, transcendentals=0
        ),
    )(everything, codes, arrived)


def update_kernel(keep, cov, arrived, col_cross, inverse, out):
    tile = cov.shape[1]
    share = 4 * GROUPS
    solved = dot(col_cross[...], inverse[...])
    for t in range(2):
        lines = arrived[:, t * share : (t + 1) * share].reshape(tile, -1)
        part = slice(t * tile, (t + 1) * tile)
        out[part] = (cov[part] - dot(lines, solved, ((1,), (1,)))) * keep[t]


def update(keep, cov, arrived, col_cross, inverse):
    return pl.pallas_call(
        update_kernel,
        out_shape=jax.ShapeDtypeStruct(cov.shape, jnp.float32),
        in_specs=[pl.BlockSpec(memory_space=pltpu.SMEM), *in_vmem(4)],
        out_specs=pl.BlockSpec(memory_space=pltpu.VMEM),
        compiler_params=params(),
    )(keep, cov, arrived, col_cross, inverse)


def body(cov, order, stations, obs_values, obs_error):
    rows, tile = cov.shape
    nobs_own = obs_values.shape[1]
    tr_size, tc_size = lax.axis_size(TR), lax.axis_size(TC)
    nobs = nobs_own * tc_size
    share = tile // tc_size
    row = lax.axis_index(TR)
    col = lax.axis_index(TC)

    tail = jnp.stack([stations[0].astype(jnp.float32), obs_error[0]], axis=1)
    packed = jnp.concatenate(
        [obs_values[0], jnp.pad(tail, ((0, 0), (0, LANES - tail.shape[1])))], axis=1
    )
    packed = jnp.broadcast_to(packed[None], (tc_size, *packed.shape))
    everything = exchange(packed, TC).reshape(nobs, tile + LANES)
    codes, rounds = make_codes(everything, order)

    def one_round(number):
        where = jnp.stack([row, col, jnp.int32(number)]).astype(jnp.int32)
        terms = exchange(make_terms(where, everything, codes, cov, tc_size), TC)
        placed, second = place_rows(where, codes, terms, tr_size)
        return gather_rows(where, codes, placed, exchange(second, TR))

    own = lax.fori_loop(1, rounds[0], lambda number, sofar: sofar + one_round(number), one_round(0))

    moves = [
        (r * tc_size + c, (c // 2) * tc_size + 2 * r + c % 2)
        for r in range(tr_size)
        for c in range(tc_size)
    ]
    moved = lax.ppermute(own[: 2 * share], ALL, moves)
    arrived = exchange(jnp.broadcast_to(own[None], (tc_size, *own.shape)), TC)
    near = jnp.broadcast_to(moved.reshape(1, 2, share, nobs), (tr_size, 2, share, nobs))
    col_cross = exchange(near.reshape(2 * tr_size, share, nobs), NEAR).reshape(tile, nobs)
    inverse = invert(everything, codes, arrived)
    places = 2 * row + jnp.arange(2, dtype=jnp.int32)
    row_order = lax.dynamic_slice_in_dim(order, 2 * row, 2)
    col_order = lax.dynamic_slice_in_dim(order, col, 1)
    keep = ((row_order > col_order) | (places == col)).astype(jnp.float32)
    return update(keep, cov, arrived, col_cross, inverse)


def solution(mesh):
    tr_size, tc_size = mesh.shape["tr"], mesh.shape["tc"]
    y_size = 8 if tc_size % 8 == 0 else tc_size
    split = Mesh(
        mesh.devices.reshape(tr_size // 2, 2, tc_size // y_size, y_size // 2, 2), ALL
    )
    return jax.shard_map(
        body,
        mesh=split,
        in_specs=(P(TR, TC), P(), P(None, TC), P(None, TC, None), P(None, TC)),
        out_specs=P(TR, TC),
        check_vma=False,
    )
```

```python
import jax
import jax.numpy as jnp
from jax import lax
from jax.experimental import pallas as pl
from jax.experimental.pallas import tpu as pltpu
from jax.sharding import Mesh
from jax.sharding import PartitionSpec as P

TR = ("z", "k")
TC = ("x", "yh", "yl")
Y = ("yh", "yl")
NEAR = ("z", "k", "yl")
ALL = ("z", "k", "x", "yh", "yl")
SLOTS = 32
PAIR_SLOTS = 48
LANES = 128
GROUPS = LANES // SLOTS
SETTLED = 1e-7

precise = lax.Precision.HIGHEST


def dot(former, latter, dims=((1,), (0,))):
    return lax.dot_general(
        former, latter, (dims, ((), ())), precision=precise, preferred_element_type=jnp.float32
    )


def halves_of(array):
    upper = array.astype(jnp.bfloat16)
    return upper, (array - upper.astype(jnp.float32)).astype(jnp.bfloat16)


def short(former, latter, dims=((1,), (0,))):
    return lax.dot_general(former, latter, (dims, ((), ())), preferred_element_type=jnp.float32)


def split_dot(former, latter, dims=((1,), (0,))):
    small = short(former[0], latter[1], dims) + short(former[1], latter[0], dims)
    return short(former[0], latter[0], dims) + small


def chosen_rows(pick, pair):
    return tuple(short(pick, part).astype(jnp.bfloat16) for part in pair)


def placing_dot(former, spots):
    upper = former.astype(jnp.bfloat16)
    rest = former - upper.astype(jnp.float32)
    middle = rest.astype(jnp.bfloat16)
    lower = (rest - middle.astype(jnp.float32)).astype(jnp.bfloat16)
    return short(upper, spots) + (short(middle, spots) + short(lower, spots))


def iota(shape, dim):
    return lax.broadcasted_iota(jnp.int32, shape, dim)


def exchange(array, axes):
    return lax.all_to_all(array, axes, 0, 0, tiled=True)


def in_vmem(count):
    return [pl.BlockSpec(memory_space=pltpu.VMEM)] * count


def params():
    return pltpu.CompilerParams(vmem_limit_bytes=48 * 1024 * 1024)


def as_row(column):
    return jnp.broadcast_to(column, (column.shape[0], LANES)).T[:1]


def pack_kernel(stations, errors, values, out):
    own, tile = values.shape
    diagonal = iota((own, own), 0) == iota((own, own), 1)
    station = jnp.sum(jnp.where(diagonal, stations[...].astype(jnp.float32), 0.0), axis=1, keepdims=True)
    error = jnp.sum(jnp.where(diagonal, errors[...], 0.0), axis=1, keepdims=True)
    tail = jnp.where(iota((own, LANES), 1) == 0, station, error)
    for place in range(out.shape[0]):
        out[place, :, :tile] = values[...]
        out[place, :, tile:] = tail


def pack(stations, errors, values, copies):
    own, tile = values.shape
    return pl.pallas_call(
        pack_kernel,
        out_shape=jax.ShapeDtypeStruct((copies, own, tile + LANES), jnp.float32),
        in_specs=in_vmem(3),
        out_specs=pl.BlockSpec(memory_space=pltpu.VMEM),
        compiler_params=params(),
    )(stations, errors, values)


def codes_kernel(everything, order_column, codes, rounds):
    nobs = everything.shape[0]
    tile = everything.shape[1] - LANES
    station = everything[:, tile : tile + 1].astype(jnp.int32)
    station_row = as_row(everything[:, tile : tile + 1]).astype(jnp.int32)
    blocks = order_column.shape[0]
    position = jnp.sum(
        jnp.where(order_column[...] == station_row, iota((blocks, nobs), 0), 0), axis=0, keepdims=True
    )
    position_column = jnp.broadcast_to(position, (LANES, nobs)).astype(jnp.float32).T[:, :1].astype(jnp.int32)
    before = iota((nobs, nobs), 0) < iota((nobs, nobs), 1)
    rank = jnp.sum(((station == station_row) & before).astype(jnp.int32), axis=0, keepdims=True)
    paired = (position_column >> 1) == (position >> 1)
    pair_rank = jnp.sum((paired & before).astype(jnp.int32), axis=0, keepdims=True)
    codes[0:1] = position
    codes[1:2] = rank
    codes[2:3] = pair_rank
    codes[3:8] = jnp.zeros((5, nobs), jnp.int32)
    rounds[0] = 1 + jnp.maximum(jnp.max(rank) // SLOTS, jnp.max(pair_rank) // PAIR_SLOTS)


def make_codes(everything, order):
    return pl.pallas_call(
        codes_kernel,
        out_shape=(
            jax.ShapeDtypeStruct((8, everything.shape[0]), jnp.int32),
            jax.ShapeDtypeStruct((1,), jnp.int32),
        ),
        in_specs=in_vmem(2),
        out_specs=(pl.BlockSpec(memory_space=pltpu.VMEM), pl.BlockSpec(memory_space=pltpu.SMEM)),
        compiler_params=params(),
    )(everything, order.reshape(-1, 1))


def slot_codes(codes, number):
    position = codes[0:1]
    slot = codes[1:2] - number * SLOTS
    code = jnp.where((slot >= 0) & (slot < SLOTS), position * SLOTS + slot, -1)
    pair_slot = codes[2:3] - number * PAIR_SLOTS
    pair_code = jnp.where(
        (pair_slot >= 0) & (pair_slot < PAIR_SLOTS), (position >> 1) * PAIR_SLOTS + pair_slot, -1
    )
    return position, code, pair_code


def terms_kernel(where, everything, codes, cov, out):
    row, col, number = where[0], where[1], where[2]
    rows, tile = cov.shape
    nobs = everything.shape[0]
    groups = out.shape[0]
    halves = tile // groups // 8
    values = everything[:, :tile]
    position, code, pair_code = slot_codes(codes, number)
    sub = iota((LANES, nobs), 0)
    pick = (code == col * SLOTS + sub % SLOTS).astype(jnp.bfloat16)
    weights = halves_of(values)
    covariance = halves_of(cov[...])
    row_terms = split_dot(covariance, chosen_rows(pick, weights), ((1,), (1,)))
    parts = halves_of(row_terms)
    pair_pick = (pair_code == row * PAIR_SLOTS + sub % PAIR_SLOTS) & (sub < 2 * PAIR_SLOTS)
    column_terms = jnp.zeros((LANES, tile), jnp.float32)
    gram_terms = jnp.zeros((nobs, LANES), jnp.float32)
    position_column = jnp.broadcast_to(position, (LANES, nobs)).astype(jnp.float32).T[:, :1]
    for t in range(2):
        place = 2 * row + t
        lines = slice(t * tile, (t + 1) * tile)
        off_diagonal = jnp.where(place != col, 1.0, 0.0)
        chosen = (pair_pick & (position == place)).astype(jnp.float32) * off_diagonal
        column_terms += split_dot(
            chosen_rows(chosen.astype(jnp.bfloat16), weights), tuple(part[lines] for part in covariance)
        )
        inside = (position_column == place.astype(jnp.float32)).astype(jnp.float32)
        gram_terms += split_dot(
            halves_of(values * inside), tuple(part[lines] for part in parts)
        )
    lane = iota((groups, 8, LANES), 2)
    shaped = row_terms.reshape(2, groups, halves, 8, LANES)
    first = jnp.zeros((groups, 8, LANES), jnp.float32)
    for t in range(2):
        for m in range(halves):
            first = jnp.where(lane // SLOTS == t * halves + m, shaped[t, :, m], first)
    out[:, :8] = first
    shaped = column_terms.T.reshape(groups, halves, 8, LANES)
    second = gram_terms.reshape(groups, 8, LANES)
    for m in range(halves):
        second = jnp.where(lane // PAIR_SLOTS == m, shaped[:, m], second)
    out[:, 8:] = second


def make_terms(where, everything, codes, cov, groups):
    return pl.pallas_call(
        terms_kernel,
        out_shape=jax.ShapeDtypeStruct((groups, 16, LANES), jnp.float32),
        in_specs=[pl.BlockSpec(memory_space=pltpu.SMEM), *in_vmem(3)],
        out_specs=pl.BlockSpec(memory_space=pltpu.VMEM),
        compiler_params=params(),
    )(where, everything, codes, cov)


def place_kernel(where, codes, arrived, placed, second):
    nobs = codes.shape[1]
    groups = arrived.shape[0]
    code = slot_codes(codes, where[2])[1]
    lane = iota((8, LANES), 1)
    parts = GROUPS + 1
    lines = [[] for _ in range(parts)]
    for g in range(groups // GROUPS):
        for part in range(parts):
            line = None
            for q in range(GROUPS):
                at, source = (part, arrived[g * GROUPS + q, :8]) if part < GROUPS else (
                    GROUPS - 1,
                    arrived[g * GROUPS + q, 8:],
                )
                shift = (q - at) * SLOTS % LANES
                turned = pltpu.roll(source, shift, 1) if shift else source
                line = turned if line is None else jnp.where(lane // SLOTS == q, turned, line)
            lines[part].append(line)
    former = jnp.concatenate([jnp.concatenate(line, axis=1) for line in lines], axis=0)
    spots = (iota((groups * SLOTS, nobs), 0) == code).astype(jnp.bfloat16)
    result = placing_dot(former, spots)
    placed[...] = result[: 8 * GROUPS]
    gram = result[8 * GROUPS :]
    for r in range(second.shape[0]):
        for t in range(2):
            second[r, t] = arrived[2 * r + t, 8:]
        for part in range(nobs // LANES):
            second[r, 2 + part] = gram[:, part * LANES : (part + 1) * LANES]


def place_rows(where, codes, arrived, tr_size):
    nobs = codes.shape[1]
    return pl.pallas_call(
        place_kernel,
        out_shape=(
            jax.ShapeDtypeStruct((8 * GROUPS, nobs), jnp.float32),
            jax.ShapeDtypeStruct((tr_size, 2 + nobs // LANES, 8, LANES), jnp.float32),
        ),
        in_specs=[pl.BlockSpec(memory_space=pltpu.SMEM), *in_vmem(2)],
        out_specs=tuple(in_vmem(2)),
        compiler_params=params(),
    )(where, codes, arrived)


def gather_kernel(where, codes, placed, arrived, out):
    nobs = codes.shape[1]
    pair_code = slot_codes(codes, where[2])[2]
    lane = iota((8, LANES), 1)
    pairs = arrived.shape[0]
    halves = GROUPS // 2
    lines = []
    for t in range(2):
        for m in range(halves):
            inside = lane // PAIR_SLOTS == m
            lines.append(
                jnp.concatenate([jnp.where(inside, arrived[r, t], 0.0) for r in range(pairs)], axis=1)
            )
    former = jnp.concatenate(lines, axis=0)
    at = iota((pairs * LANES, nobs), 0)
    within = at % LANES
    spot = jnp.where(within < 2 * PAIR_SLOTS, at // LANES * PAIR_SLOTS + within % PAIR_SLOTS, -2)
    spots = (spot == pair_code).astype(jnp.bfloat16)
    out[: 8 * GROUPS] = placed[...] + placing_dot(former, spots)
    for part in range(nobs // LANES):
        total = arrived[0, 2 + part]
        for r in range(1, pairs):
            total = total + arrived[r, 2 + part]
        out[8 * GROUPS :, part * LANES : (part + 1) * LANES] = total


def gather_rows(where, codes, placed, arrived):
    nobs = codes.shape[1]
    return pl.pallas_call(
        gather_kernel,
        out_shape=jax.ShapeDtypeStruct((8 * GROUPS + 8, nobs), jnp.float32),
        in_specs=[pl.BlockSpec(memory_space=pltpu.SMEM), *in_vmem(3)],
        out_specs=pl.BlockSpec(memory_space=pltpu.VMEM),
        compiler_params=params(),
    )(where, codes, placed, arrived)


def inverse_kernel(everything, codes, arrived, out):
    nobs = codes.shape[1]
    tile = everything.shape[1] - LANES
    gram = arrived[:, 8 * GROUPS :].reshape(nobs, nobs)
    both = gram + gram.T
    position = codes[0:1]
    position_column = jnp.broadcast_to(position, (LANES, nobs)).astype(jnp.float32).T[:, :1].astype(jnp.int32)
    errors = everything[:, tile + 1 : tile + 2]
    unit = (iota((nobs, nobs), 0) == iota((nobs, nobs), 1)).astype(jnp.float32)
    innovation = jnp.where(position == position_column, 0.5 * both, both) + unit * errors
    low = jnp.min(errors, keepdims=True)
    sums = jnp.sum(jnp.abs(innovation), axis=1, keepdims=True)
    high = jnp.maximum(jnp.max(sums, keepdims=True), low)
    ratio = (high - low) / (high + low)
    base = 2.0 / (low + high)
    square = ratio * ratio
    scale = 2.0 / (2.0 - square)
    start = (scale * base) * (2.0 * unit - base * innovation)

    def unsettled(carry):
        count, left, _, _ = carry
        return (left > SETTLED) & (count < 64)

    def step(carry):
        count, _, spread, inverse = carry
        gap = spread * spread
        grow = 2.0 / (2.0 - gap)
        shrunk = gap * 0.5 * grow
        rest = 2.0 * unit - dot(innovation, inverse)
        return count + 1, jnp.max(shrunk), shrunk, grow * dot(inverse, rest)

    first = square * 0.5 * scale
    result = lax.while_loop(unsettled, step, (jnp.int32(0), jnp.max(first), first, start))
    out[...] = result[3]


def invert(everything, codes, arrived):
    nobs = codes.shape[1]
    return pl.pallas_call(
        inverse_kernel,
        out_shape=jax.ShapeDtypeStruct((nobs, nobs), jnp.float32),
        in_specs=in_vmem(3),
        out_specs=pl.BlockSpec(memory_space=pltpu.VMEM),
        compiler_params=params(),
        cost_estimate=pl.CostEstimate(
            flops=150 * nobs**3, bytes_accessed=8 * nobs * nobs, transcendentals=0
        ),
    )(everything, codes, arrived)


def update_kernel(keep, cov, arrived, col_cross, inverse, out):
    tile = cov.shape[1]
    share = 4 * GROUPS
    solved = halves_of(split_dot(halves_of(col_cross[...]), halves_of(inverse[...])))
    for t in range(2):
        lines = arrived[:, t * share : (t + 1) * share].reshape(tile, -1)
        part = slice(t * tile, (t + 1) * tile)
        out[part] = (cov[part] - split_dot(halves_of(lines), solved, ((1,), (1,)))) * keep[t]


def update(keep, cov, arrived, col_cross, inverse):
    return pl.pallas_call(
        update_kernel,
        out_shape=jax.ShapeDtypeStruct(cov.shape, jnp.float32),
        in_specs=[pl.BlockSpec(memory_space=pltpu.SMEM), *in_vmem(4)],
        out_specs=pl.BlockSpec(memory_space=pltpu.VMEM),
        compiler_params=params(),
    )(keep, cov, arrived, col_cross, inverse)


def body(cov, order, stations, obs_values, obs_error):
    rows, tile = cov.shape
    nobs_own = obs_values.shape[1]
    tr_size, tc_size = lax.axis_size(TR), lax.axis_size(TC)
    nobs = nobs_own * tc_size
    share = tile // tc_size
    row = lax.axis_index(TR)
    col = lax.axis_index(TC)

    packed = pack(stations, obs_error, obs_values[0], tc_size)
    everything = exchange(packed, TC).reshape(nobs, tile + LANES)
    codes, rounds = make_codes(everything, order)

    def one_round(number):
        where = jnp.stack([row, col, jnp.int32(number)]).astype(jnp.int32)
        terms = exchange(make_terms(where, everything, codes, cov, tc_size), TC)
        placed, second = place_rows(where, codes, terms, tr_size)
        return gather_rows(where, codes, placed, exchange(second, TR))

    own = lax.fori_loop(1, rounds[0], lambda number, sofar: sofar + one_round(number), one_round(0))

    moves = [
        (r * tc_size + c, (c // 2) * tc_size + 2 * r + c % 2)
        for r in range(tr_size)
        for c in range(tc_size)
    ]
    moved = lax.ppermute(own[: 2 * share], ALL, moves)
    arrived = own
    for axes in (Y, "x"):
        count = lax.axis_size(axes)
        arrived = exchange(jnp.broadcast_to(arrived[None], (count, *arrived.shape)), axes)
    arrived = arrived.reshape(tc_size, *own.shape)
    moved, arrived = lax.optimization_barrier((moved, arrived))
    near = jnp.broadcast_to(moved.reshape(1, 2, share, nobs), (tr_size, 2, share, nobs))
    col_cross = exchange(near.reshape(2 * tr_size, share, nobs), NEAR).reshape(tile, nobs)
    inverse = invert(everything, codes, arrived)
    places = 2 * row + jnp.arange(2, dtype=jnp.int32)
    row_order = lax.dynamic_slice_in_dim(order, 2 * row, 2)
    col_order = lax.dynamic_slice_in_dim(order, col, 1)
    keep = ((row_order > col_order) | (places == col)).astype(jnp.float32)
    return update(keep, cov, arrived, col_cross, inverse)


def solution(mesh):
    tr_size, tc_size = mesh.shape["tr"], mesh.shape["tc"]
    y_size = 8 if tc_size % 8 == 0 else tc_size
    split = Mesh(
        mesh.devices.reshape(tr_size // 2, 2, tc_size // y_size, y_size // 2, 2), ALL
    )
    return jax.shard_map(
        body,
        mesh=split,
        in_specs=(P(TR, TC), P(), P(None, TC), P(None, TC, None), P(None, TC)),
        out_specs=P(TR, TC),
        check_vma=False,
    )
```

```python
import jax
import jax.numpy as jnp
from jax import lax
from jax.experimental import pallas as pl
from jax.experimental.pallas import tpu as pltpu
from jax.sharding import Mesh
from jax.sharding import PartitionSpec as P

TR = ("z", "k")
TC = ("x", "yh", "yl")
Y = ("yh", "yl")
NEAR = ("z", "k", "yl")
ALL = ("z", "k", "x", "yh", "yl")
SLOTS = 32
PAIR_SLOTS = 48
LANES = 128
GROUPS = LANES // SLOTS
SETTLED = 1e-7

precise = lax.Precision.HIGHEST


def dot(former, latter, dims=((1,), (0,))):
    return lax.dot_general(
        former, latter, (dims, ((), ())), precision=precise, preferred_element_type=jnp.float32
    )


def halves_of(array):
    upper = array.astype(jnp.bfloat16)
    return upper, (array - upper.astype(jnp.float32)).astype(jnp.bfloat16)


def short(former, latter, dims=((1,), (0,))):
    return lax.dot_general(former, latter, (dims, ((), ())), preferred_element_type=jnp.float32)


def split_dot(former, latter, dims=((1,), (0,))):
    return short(
        jnp.concatenate([former[0], former[1], former[0]], axis=dims[0][0]),
        jnp.concatenate([latter[0], latter[0], latter[1]], axis=dims[1][0]),
        dims,
    )


def chosen_rows(pick, pair):
    return tuple(short(pick, part).astype(jnp.bfloat16) for part in pair)


def placing_dot(former, spots):
    upper = former.astype(jnp.bfloat16)
    rest = former - upper.astype(jnp.float32)
    middle = rest.astype(jnp.bfloat16)
    lower = (rest - middle.astype(jnp.float32)).astype(jnp.bfloat16)
    return short(upper, spots) + (short(middle, spots) + short(lower, spots))


def iota(shape, dim):
    return lax.broadcasted_iota(jnp.int32, shape, dim)


def exchange(array, axes):
    return lax.all_to_all(array, axes, 0, 0, tiled=True)


def in_vmem(count):
    return [pl.BlockSpec(memory_space=pltpu.VMEM)] * count


def params():
    return pltpu.CompilerParams(vmem_limit_bytes=48 * 1024 * 1024)


def as_row(column):
    return jnp.broadcast_to(column, (column.shape[0], LANES)).T[:1]


def pack_kernel(stations_at, errors_at, values_at, out, stations, errors, values, arrived):
    copies = [
        pltpu.make_async_copy(source, held, arrived.at[number])
        for number, (source, held) in enumerate(
            ((stations_at, stations), (errors_at, errors), (values_at, values))
        )
    ]
    for copy in copies:
        copy.start()
    for copy in copies:
        copy.wait()
    own, tile = values.shape
    diagonal = iota((own, own), 0) == iota((own, own), 1)
    station = jnp.sum(jnp.where(diagonal, stations[...].astype(jnp.float32), 0.0), axis=1, keepdims=True)
    error = jnp.sum(jnp.where(diagonal, errors[...], 0.0), axis=1, keepdims=True)
    tail = jnp.where(iota((own, LANES), 1) == 0, station, error)
    for place in range(out.shape[0]):
        out[place, :, :tile] = values[...]
        out[place, :, tile:] = tail


def pack(stations, errors, values, copies):
    own, tile = values.shape
    return pl.pallas_call(
        pack_kernel,
        out_shape=jax.ShapeDtypeStruct((copies, own, tile + LANES), jnp.float32),
        in_specs=[pl.BlockSpec(memory_space=pltpu.HBM)] * 3,
        out_specs=pl.BlockSpec(memory_space=pltpu.VMEM),
        scratch_shapes=[
            pltpu.VMEM(stations.shape, jnp.int32),
            pltpu.VMEM(errors.shape, jnp.float32),
            pltpu.VMEM(values.shape, jnp.float32),
            pltpu.SemaphoreType.DMA((3,)),
        ],
        compiler_params=params(),
    )(stations, errors, values)


def codes_kernel(everything, order_column, codes, rounds):
    nobs = everything.shape[0]
    tile = everything.shape[1] - LANES
    station = everything[:, tile : tile + 1].astype(jnp.int32)
    station_row = as_row(everything[:, tile : tile + 1]).astype(jnp.int32)
    blocks = order_column.shape[0]
    position = jnp.sum(
        jnp.where(order_column[...] == station_row, iota((blocks, nobs), 0), 0), axis=0, keepdims=True
    )
    position_column = jnp.broadcast_to(position, (LANES, nobs)).astype(jnp.float32).T[:, :1].astype(jnp.int32)
    before = iota((nobs, nobs), 0) < iota((nobs, nobs), 1)
    rank = jnp.sum(((station == station_row) & before).astype(jnp.int32), axis=0, keepdims=True)
    paired = (position_column >> 1) == (position >> 1)
    pair_rank = jnp.sum((paired & before).astype(jnp.int32), axis=0, keepdims=True)
    codes[0:1] = position
    codes[1:2] = rank
    codes[2:3] = pair_rank
    codes[3:8] = jnp.zeros((5, nobs), jnp.int32)
    rounds[0] = 1 + jnp.maximum(jnp.max(rank) // SLOTS, jnp.max(pair_rank) // PAIR_SLOTS)


def make_codes(everything, order):
    return pl.pallas_call(
        codes_kernel,
        out_shape=(
            jax.ShapeDtypeStruct((8, everything.shape[0]), jnp.int32),
            jax.ShapeDtypeStruct((1,), jnp.int32),
        ),
        in_specs=in_vmem(2),
        out_specs=(pl.BlockSpec(memory_space=pltpu.VMEM), pl.BlockSpec(memory_space=pltpu.SMEM)),
        compiler_params=params(),
    )(everything, order.reshape(-1, 1))


def slot_codes(codes, number):
    position = codes[0:1]
    slot = codes[1:2] - number * SLOTS
    code = jnp.where((slot >= 0) & (slot < SLOTS), position * SLOTS + slot, -1)
    pair_slot = codes[2:3] - number * PAIR_SLOTS
    pair_code = jnp.where(
        (pair_slot >= 0) & (pair_slot < PAIR_SLOTS), (position >> 1) * PAIR_SLOTS + pair_slot, -1
    )
    return position, code, pair_code


def terms_kernel(where, everything, codes, cov, out):
    row, col, number = where[0], where[1], where[2]
    rows, tile = cov.shape
    nobs = everything.shape[0]
    groups = out.shape[0]
    halves = tile // groups // 8
    values = everything[:, :tile]
    position, code, pair_code = slot_codes(codes, number)
    sub = iota((LANES, nobs), 0)
    pick = (code == col * SLOTS + sub % SLOTS).astype(jnp.bfloat16)
    weights = halves_of(values)
    covariance = halves_of(cov[...])
    row_terms = split_dot(covariance, chosen_rows(pick, weights), ((1,), (1,)))
    parts = halves_of(row_terms)
    pair_pick = (pair_code == row * PAIR_SLOTS + sub % PAIR_SLOTS) & (sub < 2 * PAIR_SLOTS)
    column_terms = jnp.zeros((LANES, tile), jnp.float32)
    gram_terms = jnp.zeros((nobs, LANES), jnp.float32)
    position_column = jnp.broadcast_to(position, (LANES, nobs)).astype(jnp.float32).T[:, :1]
    for t in range(2):
        place = 2 * row + t
        lines = slice(t * tile, (t + 1) * tile)
        off_diagonal = jnp.where(place != col, 1.0, 0.0)
        chosen = (pair_pick & (position == place)).astype(jnp.float32) * off_diagonal
        column_terms += split_dot(
            chosen_rows(chosen.astype(jnp.bfloat16), weights), tuple(part[lines] for part in covariance)
        )
        inside = (position_column == place.astype(jnp.float32)).astype(jnp.float32)
        gram_terms += split_dot(
            halves_of(values * inside), tuple(part[lines] for part in parts)
        )
    lane = iota((groups, 8, LANES), 2)
    shaped = row_terms.reshape(2, groups, halves, 8, LANES)
    first = jnp.zeros((groups, 8, LANES), jnp.float32)
    for t in range(2):
        for m in range(halves):
            first = jnp.where(lane // SLOTS == t * halves + m, shaped[t, :, m], first)
    out[:, :8] = first
    shaped = column_terms.T.reshape(groups, halves, 8, LANES)
    second = gram_terms.reshape(groups, 8, LANES)
    for m in range(halves):
        second = jnp.where(lane // PAIR_SLOTS == m, shaped[:, m], second)
    out[:, 8:] = second


def make_terms(where, everything, codes, cov, groups):
    return pl.pallas_call(
        terms_kernel,
        out_shape=jax.ShapeDtypeStruct((groups, 16, LANES), jnp.float32),
        in_specs=[pl.BlockSpec(memory_space=pltpu.SMEM), *in_vmem(3)],
        out_specs=pl.BlockSpec(memory_space=pltpu.VMEM),
        compiler_params=params(),
    )(where, everything, codes, cov)


def place_kernel(where, codes, arrived, placed, second):
    nobs = codes.shape[1]
    groups = arrived.shape[0]
    code = slot_codes(codes, where[2])[1]
    lane = iota((8, LANES), 1)
    parts = GROUPS + 1
    lines = [[] for _ in range(parts)]
    for g in range(groups // GROUPS):
        for part in range(parts):
            line = None
            for q in range(GROUPS):
                at, source = (part, arrived[g * GROUPS + q, :8]) if part < GROUPS else (
                    GROUPS - 1,
                    arrived[g * GROUPS + q, 8:],
                )
                shift = (q - at) * SLOTS % LANES
                turned = pltpu.roll(source, shift, 1) if shift else source
                line = turned if line is None else jnp.where(lane // SLOTS == q, turned, line)
            lines[part].append(line)
    former = jnp.concatenate([jnp.concatenate(line, axis=1) for line in lines], axis=0)
    spots = (iota((groups * SLOTS, nobs), 0) == code).astype(jnp.bfloat16)
    result = placing_dot(former, spots)
    placed[...] = result[: 8 * GROUPS]
    gram = result[8 * GROUPS :]
    for r in range(second.shape[0]):
        for t in range(2):
            second[r, t] = arrived[2 * r + t, 8:]
        for part in range(nobs // LANES):
            second[r, 2 + part] = gram[:, part * LANES : (part + 1) * LANES]


def place_rows(where, codes, arrived, tr_size):
    nobs = codes.shape[1]
    return pl.pallas_call(
        place_kernel,
        out_shape=(
            jax.ShapeDtypeStruct((8 * GROUPS, nobs), jnp.float32),
            jax.ShapeDtypeStruct((tr_size, 2 + nobs // LANES, 8, LANES), jnp.float32),
        ),
        in_specs=[pl.BlockSpec(memory_space=pltpu.SMEM), *in_vmem(2)],
        out_specs=tuple(in_vmem(2)),
        compiler_params=params(),
    )(where, codes, arrived)


def gather_kernel(where, codes, placed, arrived, out):
    nobs = codes.shape[1]
    pair_code = slot_codes(codes, where[2])[2]
    lane = iota((8, LANES), 1)
    pairs = arrived.shape[0]
    halves = GROUPS // 2
    lines = []
    for t in range(2):
        for m in range(halves):
            inside = lane // PAIR_SLOTS == m
            lines.append(
                jnp.concatenate([jnp.where(inside, arrived[r, t], 0.0) for r in range(pairs)], axis=1)
            )
    former = jnp.concatenate(lines, axis=0)
    at = iota((pairs * LANES, nobs), 0)
    within = at % LANES
    spot = jnp.where(within < 2 * PAIR_SLOTS, at // LANES * PAIR_SLOTS + within % PAIR_SLOTS, -2)
    spots = (spot == pair_code).astype(jnp.bfloat16)
    out[: 8 * GROUPS] = placed[...] + placing_dot(former, spots)
    for part in range(nobs // LANES):
        total = arrived[0, 2 + part]
        for r in range(1, pairs):
            total = total + arrived[r, 2 + part]
        out[8 * GROUPS :, part * LANES : (part + 1) * LANES] = total


def gather_rows(where, codes, placed, arrived):
    nobs = codes.shape[1]
    return pl.pallas_call(
        gather_kernel,
        out_shape=jax.ShapeDtypeStruct((8 * GROUPS + 8, nobs), jnp.float32),
        in_specs=[pl.BlockSpec(memory_space=pltpu.SMEM), *in_vmem(3)],
        out_specs=pl.BlockSpec(memory_space=pltpu.VMEM),
        compiler_params=params(),
    )(where, codes, placed, arrived)


def source_of(place, away, count):
    return lax.rem(place + count - away, count)


def inverse_kernel(where, everything, codes, *refs):
    pieces, (out, grid, rest) = refs[:-3], refs[-3:]
    for away, piece in enumerate(pieces):
        lines = piece[:, 8 * GROUPS :].reshape(-1, codes.shape[1])
        start = source_of(where[3], away, len(pieces)) * lines.shape[0]
        grid[pl.ds(pl.multiple_of(start, 8), lines.shape[0])] = lines
    nobs = codes.shape[1]
    tile = everything.shape[1] - LANES
    gram = grid[...]
    both = gram + gram.T
    position = codes[0:1]
    position_column = jnp.broadcast_to(position, (LANES, nobs)).astype(jnp.float32).T[:, :1].astype(jnp.int32)
    errors = everything[:, tile + 1 : tile + 2]
    unit = (iota((nobs, nobs), 0) == iota((nobs, nobs), 1)).astype(jnp.float32)
    innovation = jnp.where(position == position_column, 0.5 * both, both) + unit * errors
    low = jnp.min(errors, keepdims=True)
    sums = jnp.sum(jnp.abs(innovation), axis=1, keepdims=True)
    high = jnp.maximum(jnp.max(sums, keepdims=True), low)
    ratio = (high - low) / (high + low)
    base = 2.0 / (low + high)
    square = ratio * ratio
    scale = 2.0 / (2.0 - square)
    out[...] = (scale * base) * (2.0 * unit - base * innovation)
    cautious = jnp.max(high - 1000.0 * low) > 0.0
    parts = halves_of(innovation)

    def unsettled(carry):
        count, left, _ = carry
        return (left > SETTLED) & (count < 64)

    def step(carry):
        count, left, spread = carry
        gap = spread * spread
        grow = 2.0 / (2.0 - gap)
        shrunk = gap * 0.5 * grow
        exact = cautious | (left < 1e-3)

        @pl.when(exact)
        def _():
            rest[...] = unit - dot(innovation, out[...])

        @pl.when(jnp.logical_not(exact))
        def _():
            rest[...] = unit - split_dot(parts, halves_of(out[...]))

        @pl.when(cautious)
        def _():
            out[...] = grow * (out[...] + dot(out[...], rest[...]))

        @pl.when(jnp.logical_not(cautious))
        def _():
            out[...] = grow * (out[...] + split_dot(halves_of(out[...]), halves_of(rest[...])))

        return count + 1, jnp.max(shrunk), shrunk

    first = square * 0.5 * scale
    lax.while_loop(unsettled, step, (jnp.int32(0), jnp.max(first), first))


def invert(where, everything, codes, pieces):
    nobs = codes.shape[1]
    return pl.pallas_call(
        inverse_kernel,
        out_shape=jax.ShapeDtypeStruct((nobs, nobs), jnp.float32),
        in_specs=[pl.BlockSpec(memory_space=pltpu.SMEM), *in_vmem(2 + len(pieces))],
        out_specs=pl.BlockSpec(memory_space=pltpu.VMEM),
        scratch_shapes=[pltpu.VMEM((nobs, nobs), jnp.float32)] * 2,
        compiler_params=params(),
        cost_estimate=pl.CostEstimate(
            flops=1500 * nobs**3, bytes_accessed=8 * nobs * nobs, transcendentals=0
        ),
    )(where, everything, codes, *pieces)


def update_kernel(where, keep, cov, col_cross, inverse, *refs):
    pieces, (out, held, left) = refs[:-3], refs[-3:]
    tile = cov.shape[1]
    share = 4 * GROUPS
    nobs = inverse.shape[0]
    solved = split_dot(halves_of(inverse[...]), halves_of(col_cross[...]), ((1,), (1,)))
    upper, lower = halves_of(solved)
    latter = jnp.concatenate([upper, upper, lower], axis=0)
    size = tile // len(pieces)
    copies = []
    for away, piece in enumerate(pieces):
        source = source_of(where[3], away, len(pieces))
        lines = [piece[:, t * share : (t + 1) * share].reshape(size, nobs) for t in range(2)]
        upper, lower = halves_of(jnp.concatenate(lines, axis=0))
        change = short(jnp.concatenate([upper, lower, upper], axis=1), latter)
        for t in range(2):
            part = pl.ds(pl.multiple_of(t * tile + source * size, 8), size)
            number = len(copies)
            held[number] = (cov[part] - change[t * size : (t + 1) * size]) * keep[t]
            copies.append(pltpu.make_async_copy(held.at[number], out.at[part], left.at[number]))
            copies[-1].start()
    for copy in copies:
        copy.wait()


def update(where, keep, cov, col_cross, inverse, pieces):
    tile = cov.shape[1]
    count = 2 * len(pieces)
    return pl.pallas_call(
        update_kernel,
        out_shape=jax.ShapeDtypeStruct(cov.shape, jnp.float32),
        in_specs=[pl.BlockSpec(memory_space=pltpu.SMEM)] * 2 + in_vmem(3 + len(pieces)),
        out_specs=pl.BlockSpec(memory_space=pl.ANY),
        scratch_shapes=[
            pltpu.VMEM((count, 2 * tile // count, tile), jnp.float32),
            pltpu.SemaphoreType.DMA((count,)),
        ],
        compiler_params=params(),
    )(where, keep, cov, col_cross, inverse, *pieces)


def body(cov, order, stations, obs_values, obs_error):
    rows, tile = cov.shape
    nobs_own = obs_values.shape[1]
    tr_size, tc_size = lax.axis_size(TR), lax.axis_size(TC)
    nobs = nobs_own * tc_size
    share = tile // tc_size
    row = lax.axis_index(TR)
    col = lax.axis_index(TC)

    packed = pack(stations, obs_error, obs_values[0], tc_size)
    everything = exchange(packed, TC).reshape(nobs, tile + LANES)
    codes, rounds = make_codes(everything, order)

    def place_of(number):
        place = jnp.stack([row, col, jnp.int32(number), lax.axis_index("x")])
        return place.astype(jnp.int32)

    def one_round(number):
        where = place_of(number)
        terms = exchange(make_terms(where, everything, codes, cov, tc_size), TC)
        placed, second = place_rows(where, codes, terms, tr_size)
        return gather_rows(where, codes, placed, exchange(second, TR))

    own = lax.fori_loop(1, rounds[0], lambda number, sofar: sofar + one_round(number), one_round(0))

    moves = [
        (r * tc_size + c, (c // 2) * tc_size + 2 * r + c % 2)
        for r in range(tr_size)
        for c in range(tc_size)
    ]
    moved = lax.ppermute(own[: 2 * share], ALL, moves)
    y_size, x_size = lax.axis_size(Y), lax.axis_size("x")
    near_rows = exchange(jnp.broadcast_to(own[None], (y_size, *own.shape)), Y)
    moved, near_rows = lax.optimization_barrier((moved, near_rows))
    pieces = [near_rows] + [
        lax.ppermute(near_rows, "x", [(x, (x + away) % x_size) for x in range(x_size)])
        for away in range(1, x_size)
    ]
    near = jnp.broadcast_to(moved.reshape(1, 2, share, nobs), (tr_size, 2, share, nobs))
    col_cross = exchange(near.reshape(2 * tr_size, share, nobs), NEAR).reshape(tile, nobs)
    inverse = invert(place_of(0), everything, codes, pieces)
    places = 2 * row + jnp.arange(2, dtype=jnp.int32)
    row_order = lax.dynamic_slice_in_dim(order, 2 * row, 2)
    col_order = lax.dynamic_slice_in_dim(order, col, 1)
    keep = ((row_order > col_order) | (places == col)).astype(jnp.float32)
    return update(place_of(0), keep, cov, col_cross, inverse, pieces)


def solution(mesh):
    tr_size, tc_size = mesh.shape["tr"], mesh.shape["tc"]
    y_size = 8 if tc_size % 8 == 0 else tc_size
    split = Mesh(
        mesh.devices.reshape(tr_size // 2, 2, tc_size // y_size, y_size // 2, 2), ALL
    )
    return jax.shard_map(
        body,
        mesh=split,
        in_specs=(P(TR, TC), P(), P(None, TC), P(None, TC, None), P(None, TC)),
        out_specs=P(TR, TC),
        check_vma=False,
    )
```

```python
import jax
import jax.numpy as jnp
from jax import lax
from jax.experimental import pallas as pl
from jax.experimental.pallas import tpu as pltpu
from jax.sharding import Mesh
from jax.sharding import PartitionSpec as P

TR = ("z", "k")
TC = ("x", "yh", "yl")
Y = ("yh", "yl")
ALL = ("z", "k", "x", "yh", "yl")
SLOTS = 32
PAIR_SLOTS = 48
LANES = 128
GROUPS = LANES // SLOTS
SETTLED = 1e-7

precise = lax.Precision.HIGHEST


def dot(former, latter, dims=((1,), (0,))):
    return lax.dot_general(
        former, latter, (dims, ((), ())), precision=precise, preferred_element_type=jnp.float32
    )


def halves_of(array):
    upper = array.astype(jnp.bfloat16)
    return upper, (array - upper.astype(jnp.float32)).astype(jnp.bfloat16)


def short(former, latter, dims=((1,), (0,))):
    return lax.dot_general(former, latter, (dims, ((), ())), preferred_element_type=jnp.float32)


def split_dot(former, latter, dims=((1,), (0,))):
    return short(
        jnp.concatenate([former[0], former[1], former[0]], axis=dims[0][0]),
        jnp.concatenate([latter[0], latter[0], latter[1]], axis=dims[1][0]),
        dims,
    )


def chosen_rows(pick, pair):
    return tuple(short(pick, part).astype(jnp.bfloat16) for part in pair)


def placing_dot(former, spots):
    upper = former.astype(jnp.bfloat16)
    rest = former - upper.astype(jnp.float32)
    middle = rest.astype(jnp.bfloat16)
    lower = (rest - middle.astype(jnp.float32)).astype(jnp.bfloat16)
    return short(upper, spots) + (short(middle, spots) + short(lower, spots))


def iota(shape, dim):
    return lax.broadcasted_iota(jnp.int32, shape, dim)


def exchange(array, axes):
    return lax.all_to_all(array, axes, 0, 0, tiled=True)


def in_vmem(count):
    return [pl.BlockSpec(memory_space=pltpu.VMEM)] * count


def params():
    return pltpu.CompilerParams(vmem_limit_bytes=48 * 1024 * 1024)


def as_row(column):
    return jnp.broadcast_to(column, (column.shape[0], LANES)).T[:1]


def pack_kernel(core, stations_at, errors_at, values_at, out, stations, errors, values, arrived):
    own, width = values.shape
    cells = pl.ds(pl.multiple_of(core[0] * width, LANES), width)
    copies = [
        pltpu.make_async_copy(source, held, arrived.at[number])
        for number, (source, held) in enumerate(
            ((stations_at, stations), (errors_at, errors), (values_at.at[:, cells], values))
        )
    ]
    for copy in copies:
        copy.start()
    for copy in copies:
        copy.wait()
    diagonal = iota((own, own), 0) == iota((own, own), 1)
    station = jnp.sum(jnp.where(diagonal, stations[...].astype(jnp.float32), 0.0), axis=1, keepdims=True)
    error = jnp.sum(jnp.where(diagonal, errors[...], 0.0), axis=1, keepdims=True)
    tail = jnp.where(iota((own, LANES), 1) == 0, station, error)
    for place in range(out.shape[0]):
        out[place, :, :width] = values[...]
        out[place, :, width:] = tail


def pack(core, stations, errors, values, copies):
    own, tile = values.shape
    return pl.pallas_call(
        pack_kernel,
        out_shape=jax.ShapeDtypeStruct((copies, own, tile // 2 + LANES), jnp.float32),
        in_specs=[pl.BlockSpec(memory_space=pltpu.SMEM)] + [pl.BlockSpec(memory_space=pltpu.HBM)] * 3,
        out_specs=pl.BlockSpec(memory_space=pltpu.VMEM),
        scratch_shapes=[
            pltpu.VMEM(stations.shape, jnp.int32),
            pltpu.VMEM(errors.shape, jnp.float32),
            pltpu.VMEM((own, tile // 2), jnp.float32),
            pltpu.SemaphoreType.DMA((3,)),
        ],
        compiler_params=pltpu.CompilerParams(vmem_limit_bytes=62 * 1024 * 1024),
    )(core, stations, errors, values)


def codes_kernel(everything, order_column, codes, rounds):
    nobs = everything.shape[1]
    width = everything.shape[2] - LANES
    station = everything[0, :, width : width + 1].astype(jnp.int32)
    station_row = as_row(everything[0, :, width : width + 1]).astype(jnp.int32)
    blocks = order_column.shape[0]
    position = jnp.sum(
        jnp.where(order_column[...] == station_row, iota((blocks, nobs), 0), 0), axis=0, keepdims=True
    )
    position_column = jnp.broadcast_to(position, (LANES, nobs)).astype(jnp.float32).T[:, :1].astype(jnp.int32)
    before = iota((nobs, nobs), 0) < iota((nobs, nobs), 1)
    rank = jnp.sum(((station == station_row) & before).astype(jnp.int32), axis=0, keepdims=True)
    paired = (position_column >> 1) == (position >> 1)
    pair_rank = jnp.sum((paired & before).astype(jnp.int32), axis=0, keepdims=True)
    codes[0:1] = position
    codes[1:2] = rank
    codes[2:3] = pair_rank
    codes[3:8] = jnp.zeros((5, nobs), jnp.int32)
    rounds[0] = 1 + jnp.maximum(jnp.max(rank) // SLOTS, jnp.max(pair_rank) // PAIR_SLOTS)


def make_codes(everything, order):
    return pl.pallas_call(
        codes_kernel,
        out_shape=(
            jax.ShapeDtypeStruct((8, everything.shape[1]), jnp.int32),
            jax.ShapeDtypeStruct((1,), jnp.int32),
        ),
        in_specs=in_vmem(2),
        out_specs=(pl.BlockSpec(memory_space=pltpu.VMEM), pl.BlockSpec(memory_space=pltpu.SMEM)),
        compiler_params=params(),
    )(everything, order.reshape(-1, 1))


def slot_codes(codes, number):
    position = codes[0:1]
    slot = codes[1:2] - number * SLOTS
    code = jnp.where((slot >= 0) & (slot < SLOTS), position * SLOTS + slot, -1)
    pair_slot = codes[2:3] - number * PAIR_SLOTS
    pair_code = jnp.where(
        (pair_slot >= 0) & (pair_slot < PAIR_SLOTS), (position >> 1) * PAIR_SLOTS + pair_slot, -1
    )
    return position, code, pair_code


def terms_kernel(where, everything, codes, cov, out):
    row, col, number = where[0], where[1], where[2]
    rows, tile = cov.shape
    nobs = everything.shape[1]
    groups = out.shape[0]
    values = jnp.concatenate([everything[part, :, : tile // 2] for part in range(2)], axis=1)
    position, code, pair_code = slot_codes(codes, number)
    sub = iota((LANES, nobs), 0)
    pick = (code == col * SLOTS + sub % SLOTS).astype(jnp.bfloat16)
    weights = halves_of(values)
    covariance = halves_of(cov[...])
    row_terms = split_dot(covariance, chosen_rows(pick, weights), ((1,), (1,)))
    parts = halves_of(row_terms)
    pair_pick = (pair_code == row * PAIR_SLOTS + sub % PAIR_SLOTS) & (sub < 2 * PAIR_SLOTS)
    column_terms = jnp.zeros((LANES, tile), jnp.float32)
    gram_terms = jnp.zeros((nobs, LANES), jnp.float32)
    position_column = jnp.broadcast_to(position, (LANES, nobs)).astype(jnp.float32).T[:, :1]
    for t in range(2):
        place = 2 * row + t
        lines = slice(t * tile, (t + 1) * tile)
        off_diagonal = jnp.where(place != col, 1.0, 0.0)
        chosen = (pair_pick & (position == place)).astype(jnp.float32) * off_diagonal
        column_terms += split_dot(
            chosen_rows(chosen.astype(jnp.bfloat16), weights), tuple(part[lines] for part in covariance)
        )
        inside = (position_column == place.astype(jnp.float32)).astype(jnp.float32)
        gram_terms += split_dot(
            halves_of(values * inside), tuple(part[lines] for part in parts)
        )
    lane = iota((groups, 8, LANES), 2)
    shaped = row_terms.reshape(groups, GROUPS, 8, LANES)
    first = shaped[:, 0]
    for m in range(1, GROUPS):
        first = jnp.where(lane // SLOTS == m, shaped[:, m], first)
    out[:, :8] = first
    owners = groups // 2
    shaped = column_terms.T.reshape(owners, 2, 2, 8, LANES)
    lane = iota((owners, 8, LANES), 2)
    gram = gram_terms.reshape(2, owners, 8, LANES)
    for part in range(2):
        second = jnp.where(lane // PAIR_SLOTS == 0, shaped[:, part, 0], shaped[:, part, 1])
        for side in range(2):
            out[side * owners : (side + 1) * owners, 8 + 8 * part : 16 + 8 * part] = (
                jnp.where(lane < 2 * PAIR_SLOTS, second, gram[side]) if part == 0 else second
            )


def make_terms(where, everything, codes, cov, groups):
    return pl.pallas_call(
        terms_kernel,
        out_shape=jax.ShapeDtypeStruct((groups, 24, LANES), jnp.float32),
        in_specs=[pl.BlockSpec(memory_space=pltpu.SMEM), *in_vmem(3)],
        out_specs=pl.BlockSpec(memory_space=pltpu.VMEM),
        compiler_params=params(),
    )(where, everything, codes, cov)


def place_kernel(where, codes, arrived, placed, second):
    nobs = codes.shape[1]
    groups = arrived.shape[0]
    code = slot_codes(codes, where[2])[1]
    lane = iota((8, LANES), 1)
    parts = GROUPS + 1
    lines = [[] for _ in range(parts)]
    for g in range(groups // GROUPS):
        for part in range(parts):
            line = None
            for q in range(GROUPS):
                at, source = (part, arrived[g * GROUPS + q, :8]) if part < GROUPS else (
                    GROUPS - 1,
                    arrived[g * GROUPS + q, 8:16],
                )
                shift = (q - at) * SLOTS % LANES
                turned = pltpu.roll(source, shift, 1) if shift else source
                line = turned if line is None else jnp.where(lane // SLOTS == q, turned, line)
            lines[part].append(line)
    former = jnp.concatenate([jnp.concatenate(line, axis=1) for line in lines], axis=0)
    spots = (iota((groups * SLOTS, nobs), 0) == code).astype(jnp.bfloat16)
    result = placing_dot(former, spots)
    placed[...] = result[: 8 * GROUPS]
    gram = result[8 * GROUPS :]
    side = jnp.where(where[1] >= groups // 2, 1, 0)
    for r in range(second.shape[0]):
        for part in range(2):
            second[r, part] = arrived[2 * r + side, 8 + 8 * part : 16 + 8 * part]
        for part in range(nobs // LANES):
            second[r, 2 + part] = gram[:, part * LANES : (part + 1) * LANES]


def place_rows(where, codes, arrived, tr_size):
    nobs = codes.shape[1]
    return pl.pallas_call(
        place_kernel,
        out_shape=(
            jax.ShapeDtypeStruct((8 * GROUPS, nobs), jnp.float32),
            jax.ShapeDtypeStruct((tr_size, 2 + nobs // LANES, 8, LANES), jnp.float32),
        ),
        in_specs=[pl.BlockSpec(memory_space=pltpu.SMEM), *in_vmem(2)],
        out_specs=tuple(in_vmem(2)),
        compiler_params=params(),
    )(where, codes, arrived)


def gather_kernel(where, codes, placed, arrived, out):
    nobs = codes.shape[1]
    pair_code = slot_codes(codes, where[2])[2]
    lane = iota((8, LANES), 1)
    pairs = arrived.shape[0]
    halves = GROUPS // 2
    lines = []
    for t in range(2):
        for m in range(halves):
            inside = lane // PAIR_SLOTS == m
            lines.append(
                jnp.concatenate([jnp.where(inside, arrived[r, t], 0.0) for r in range(pairs)], axis=1)
            )
    former = jnp.concatenate(lines, axis=0)
    at = iota((pairs * LANES, nobs), 0)
    within = at % LANES
    spot = jnp.where(within < 2 * PAIR_SLOTS, at // LANES * PAIR_SLOTS + within % PAIR_SLOTS, -2)
    spots = (spot == pair_code).astype(jnp.bfloat16)
    out[: 8 * GROUPS] = placed[...] + placing_dot(former, spots)
    for part in range(nobs // LANES):
        total = arrived[0, 2 + part]
        for r in range(1, pairs):
            total = total + arrived[r, 2 + part]
        out[8 * GROUPS :, part * LANES : (part + 1) * LANES] = total


def gather_rows(where, codes, placed, arrived):
    nobs = codes.shape[1]
    return pl.pallas_call(
        gather_kernel,
        out_shape=jax.ShapeDtypeStruct((8 * GROUPS + 8, nobs), jnp.float32),
        in_specs=[pl.BlockSpec(memory_space=pltpu.SMEM), *in_vmem(3)],
        out_specs=pl.BlockSpec(memory_space=pltpu.VMEM),
        compiler_params=params(),
    )(where, codes, placed, arrived)


def source_of(place, away, count):
    return lax.rem(place + count - away, count)


def inverse_kernel(where, everything, codes, *refs):
    pieces, (out, grid, rest) = refs[:-3], refs[-3:]
    for away, piece in enumerate(pieces):
        lines = piece[:, 8 * GROUPS :].reshape(-1, codes.shape[1])
        start = source_of(where[3], away, len(pieces)) * lines.shape[0]
        grid[pl.ds(pl.multiple_of(start, 8), lines.shape[0])] = lines
    nobs = codes.shape[1]
    width = everything.shape[2] - LANES
    gram = grid[...]
    both = gram + gram.T
    position = codes[0:1]
    position_column = jnp.broadcast_to(position, (LANES, nobs)).astype(jnp.float32).T[:, :1].astype(jnp.int32)
    errors = everything[0, :, width + 1 : width + 2]
    unit = (iota((nobs, nobs), 0) == iota((nobs, nobs), 1)).astype(jnp.float32)
    innovation = jnp.where(position == position_column, 0.5 * both, both) + unit * errors
    low = jnp.min(errors, keepdims=True)
    sums = jnp.sum(jnp.abs(innovation), axis=1, keepdims=True)
    high = jnp.maximum(jnp.max(sums, keepdims=True), low)
    ratio = (high - low) / (high + low)
    base = 2.0 / (low + high)
    square = ratio * ratio
    scale = 2.0 / (2.0 - square)
    out[...] = (scale * base) * (2.0 * unit - base * innovation)
    cautious = jnp.max(high - 1000.0 * low) > 0.0
    parts = halves_of(innovation)

    def unsettled(carry):
        count, left, _ = carry
        return (left > SETTLED) & (count < 64)

    def step(carry):
        count, left, spread = carry
        gap = spread * spread
        grow = 2.0 / (2.0 - gap)
        shrunk = gap * 0.5 * grow
        exact = cautious | (left < 1e-3)

        @pl.when(exact)
        def _():
            rest[...] = unit - dot(innovation, out[...])

        @pl.when(jnp.logical_not(exact))
        def _():
            rest[...] = unit - split_dot(parts, halves_of(out[...]))

        @pl.when(cautious)
        def _():
            out[...] = grow * (out[...] + dot(out[...], rest[...]))

        @pl.when(jnp.logical_not(cautious))
        def _():
            out[...] = grow * (out[...] + split_dot(halves_of(out[...]), halves_of(rest[...])))

        return count + 1, jnp.max(shrunk), shrunk

    first = square * 0.5 * scale
    lax.while_loop(unsettled, step, (jnp.int32(0), jnp.max(first), first))


def invert(where, everything, codes, pieces):
    nobs = codes.shape[1]
    return pl.pallas_call(
        inverse_kernel,
        out_shape=jax.ShapeDtypeStruct((nobs, nobs), jnp.float32),
        in_specs=[pl.BlockSpec(memory_space=pltpu.SMEM), *in_vmem(2 + len(pieces))],
        out_specs=pl.BlockSpec(memory_space=pltpu.VMEM),
        scratch_shapes=[pltpu.VMEM((nobs, nobs), jnp.float32)] * 2,
        compiler_params=params(),
        cost_estimate=pl.CostEstimate(
            flops=1500 * nobs**3, bytes_accessed=8 * nobs * nobs, transcendentals=0
        ),
    )(where, everything, codes, *pieces)


def update_kernel(where, keep, cov, col_cross, inverse, *refs):
    pieces, (out, held, left) = refs[:-3], refs[-3:]
    tile = cov.shape[1]
    nobs = inverse.shape[0]
    lines = jnp.swapaxes(col_cross[...], 0, 1).reshape(tile, nobs)
    solved = split_dot(halves_of(inverse[...]), halves_of(lines), ((1,), (1,)))
    upper, lower = halves_of(solved)
    latter = jnp.concatenate([upper, upper, lower], axis=0)
    size = 2 * tile // len(pieces)
    copies = []
    for away, piece in enumerate(pieces):
        source = source_of(where[3], away, len(pieces))
        upper, lower = halves_of(piece[:, : 8 * GROUPS].reshape(size, nobs))
        change = short(jnp.concatenate([upper, lower, upper], axis=1), latter)
        part = pl.ds(pl.multiple_of(source * size, 8), size)
        kept = keep[lax.div(source * size, tile)]
        held[away] = (cov[part] - change) * kept
        copies.append(pltpu.make_async_copy(held.at[away], out.at[part], left.at[away]))
        copies[-1].start()
    for copy in copies:
        copy.wait()


def update(where, keep, cov, col_cross, inverse, pieces):
    tile = cov.shape[1]
    count = len(pieces)
    return pl.pallas_call(
        update_kernel,
        out_shape=jax.ShapeDtypeStruct(cov.shape, jnp.float32),
        in_specs=[pl.BlockSpec(memory_space=pltpu.SMEM)] * 2 + in_vmem(3 + len(pieces)),
        out_specs=pl.BlockSpec(memory_space=pl.ANY),
        scratch_shapes=[
            pltpu.VMEM((count, 2 * tile // count, tile), jnp.float32),
            pltpu.SemaphoreType.DMA((count,)),
        ],
        compiler_params=params(),
    )(where, keep, cov, col_cross, inverse, *pieces)


def body(cov, order, stations, obs_values, obs_error):
    rows, tile = cov.shape
    nobs_own = obs_values.shape[1]
    tr_size, tc_size = lax.axis_size(TR), lax.axis_size(TC)
    nobs = nobs_own * tc_size
    row = lax.axis_index(TR)
    col = lax.axis_index(TC)

    core = lax.axis_index("k").astype(jnp.int32).reshape(1)
    packed = pack(core, stations, obs_error, obs_values[0], tc_size)
    everything = lax.all_gather(exchange(packed, TC), "k").reshape(2, nobs, tile // 2 + LANES)
    codes, rounds = make_codes(everything, order)

    def place_of(number):
        place = jnp.stack([row, col, jnp.int32(number), lax.axis_index("x")])
        return place.astype(jnp.int32)

    def one_round(number):
        where = place_of(number)
        terms = exchange(make_terms(where, everything, codes, cov, tc_size), TC)
        placed, second = place_rows(where, codes, terms, tr_size)
        return gather_rows(where, codes, placed, exchange(second, TR))

    own = lax.fori_loop(1, rounds[0], lambda number, sofar: sofar + one_round(number), one_round(0))

    moves = [
        (r * tc_size + c, c % (tc_size // 2) * tc_size + 2 * r + c // (tc_size // 2))
        for r in range(tr_size)
        for c in range(tc_size)
    ]
    moved = lax.ppermute(own[: 8 * GROUPS], ALL, moves)
    y_size, x_size = lax.axis_size(Y), lax.axis_size("x")
    near_rows = exchange(jnp.broadcast_to(own[None], (y_size, *own.shape)), Y)
    moved, near_rows = lax.optimization_barrier((moved, near_rows))
    pieces = [near_rows] + [
        lax.ppermute(near_rows, "x", [(x, (x + away) % x_size) for x in range(x_size)])
        for away in range(1, x_size)
    ]
    col_cross = exchange(jnp.broadcast_to(moved[None], (tr_size // 2, *moved.shape)), "z")
    inverse = invert(place_of(0), everything, codes, pieces)
    col_cross, inverse = lax.optimization_barrier((col_cross, inverse))
    col_cross = lax.all_gather(col_cross, "k")
    places = 2 * row + jnp.arange(2, dtype=jnp.int32)
    row_order = lax.dynamic_slice_in_dim(order, 2 * row, 2)
    col_order = lax.dynamic_slice_in_dim(order, col, 1)
    keep = ((row_order > col_order) | (places == col)).astype(jnp.float32)
    return update(place_of(0), keep, cov, col_cross, inverse, pieces)


def solution(mesh):
    tr_size, tc_size = mesh.shape["tr"], mesh.shape["tc"]
    y_size = 8 if tc_size % 8 == 0 else tc_size
    split = Mesh(
        mesh.devices.reshape(tr_size // 2, 2, tc_size // y_size, y_size // 2, 2), ALL
    )
    return jax.shard_map(
        body,
        mesh=split,
        in_specs=(P(TR, TC), P(), P(None, TC), P(None, TC, None), P(None, TC)),
        out_specs=P(TR, TC),
        check_vma=False,
    )
```

```python
import jax
import jax.numpy as jnp
from jax import lax
from jax.experimental import pallas as pl
from jax.experimental.pallas import tpu as pltpu
from jax.sharding import Mesh
from jax.sharding import PartitionSpec as P

TR = ("z", "k")
TC = ("x", "yh", "yl")
Y = ("yh", "yl")
ALL = ("z", "k", "x", "yh", "yl")
LANES = 128
SPAN = 32
GROUPS = LANES // SPAN
SLOTS = 24
PAIR_SLOTS = 32
SETTLED = 1e-7

precise = lax.Precision.HIGHEST


def dot(former, latter, dims=((1,), (0,))):
    return lax.dot_general(
        former, latter, (dims, ((), ())), precision=precise, preferred_element_type=jnp.float32
    )


def halves_of(array):
    upper = array.astype(jnp.bfloat16)
    return upper, (array - upper.astype(jnp.float32)).astype(jnp.bfloat16)


def short(former, latter, dims=((1,), (0,))):
    return lax.dot_general(former, latter, (dims, ((), ())), preferred_element_type=jnp.float32)


def split_dot(former, latter, dims=((1,), (0,))):
    return short(
        jnp.concatenate([former[0], former[1], former[0]], axis=dims[0][0]),
        jnp.concatenate([latter[0], latter[0], latter[1]], axis=dims[1][0]),
        dims,
    )


def chosen_rows(pick, pair):
    return tuple(short(pick, part).astype(jnp.bfloat16) for part in pair)


def placing_dot(former, spots):
    upper = former.astype(jnp.bfloat16)
    rest = former - upper.astype(jnp.float32)
    middle = rest.astype(jnp.bfloat16)
    lower = (rest - middle.astype(jnp.float32)).astype(jnp.bfloat16)
    return short(upper, spots) + (short(middle, spots) + short(lower, spots))


def iota(shape, dim):
    return lax.broadcasted_iota(jnp.int32, shape, dim)


def exchange(array, axes):
    return lax.all_to_all(array, axes, 0, 0, tiled=True)


def in_vmem(count):
    return [pl.BlockSpec(memory_space=pltpu.VMEM)] * count


def params():
    return pltpu.CompilerParams(vmem_limit_bytes=48 * 1024 * 1024)


def as_row(column):
    return jnp.broadcast_to(column, (column.shape[0], LANES)).T[:1]


def pack_kernel(core, stations_at, errors_at, values_at, out, stations, errors, values, arrived):
    own, width = values.shape
    cells = pl.ds(pl.multiple_of(core[0] * width, LANES), width)
    copies = [
        pltpu.make_async_copy(source, held, arrived.at[number])
        for number, (source, held) in enumerate(
            ((stations_at, stations), (errors_at, errors), (values_at.at[:, cells], values))
        )
    ]
    for copy in copies:
        copy.start()
    for copy in copies:
        copy.wait()
    diagonal = iota((own, own), 0) == iota((own, own), 1)
    station = jnp.sum(jnp.where(diagonal, stations[...].astype(jnp.float32), 0.0), axis=1, keepdims=True)
    error = jnp.sum(jnp.where(diagonal, errors[...], 0.0), axis=1, keepdims=True)
    tail = jnp.where(iota((own, LANES), 1) == 0, station, error)
    for place in range(out.shape[0]):
        out[place, :, :width] = values[...]
        out[place, :, width:] = tail


def pack(core, stations, errors, values, copies):
    own, tile = values.shape
    return pl.pallas_call(
        pack_kernel,
        out_shape=jax.ShapeDtypeStruct((copies, own, tile // 2 + LANES), jnp.float32),
        in_specs=[pl.BlockSpec(memory_space=pltpu.SMEM)] + [pl.BlockSpec(memory_space=pltpu.HBM)] * 3,
        out_specs=pl.BlockSpec(memory_space=pltpu.VMEM),
        scratch_shapes=[
            pltpu.VMEM(stations.shape, jnp.int32),
            pltpu.VMEM(errors.shape, jnp.float32),
            pltpu.VMEM((own, tile // 2), jnp.float32),
            pltpu.SemaphoreType.DMA((3,)),
        ],
        compiler_params=pltpu.CompilerParams(vmem_limit_bytes=62 * 1024 * 1024),
    )(core, stations, errors, values)


def codes_kernel(everything, order_column, codes, rounds):
    nobs = everything.shape[1]
    width = everything.shape[2] - LANES
    station = everything[0, :, width : width + 1].astype(jnp.int32)
    station_row = as_row(everything[0, :, width : width + 1]).astype(jnp.int32)
    blocks = order_column.shape[0]
    position = jnp.sum(
        jnp.where(order_column[...] == station_row, iota((blocks, nobs), 0), 0), axis=0, keepdims=True
    )
    position_column = jnp.broadcast_to(position, (LANES, nobs)).astype(jnp.float32).T[:, :1].astype(jnp.int32)
    before = iota((nobs, nobs), 0) < iota((nobs, nobs), 1)
    rank = jnp.sum(((station == station_row) & before).astype(jnp.int32), axis=0, keepdims=True)
    paired = (position_column >> 1) == (position >> 1)
    pair_rank = jnp.sum((paired & before).astype(jnp.int32), axis=0, keepdims=True)
    codes[0:1] = position
    codes[1:2] = rank
    codes[2:3] = pair_rank
    codes[3:8] = jnp.zeros((5, nobs), jnp.int32)
    rounds[0] = 1 + jnp.maximum(jnp.max(rank) // SLOTS, jnp.max(pair_rank) // PAIR_SLOTS)


def make_codes(everything, order):
    return pl.pallas_call(
        codes_kernel,
        out_shape=(
            jax.ShapeDtypeStruct((8, everything.shape[1]), jnp.int32),
            jax.ShapeDtypeStruct((1,), jnp.int32),
        ),
        in_specs=in_vmem(2),
        out_specs=(pl.BlockSpec(memory_space=pltpu.VMEM), pl.BlockSpec(memory_space=pltpu.SMEM)),
        compiler_params=params(),
    )(everything, order.reshape(-1, 1))


def slot_codes(codes, number):
    position = codes[0:1]
    slot = codes[1:2] - number * SLOTS
    code = jnp.where((slot >= 0) & (slot < SLOTS), position * SPAN + slot, -1)
    pair_slot = codes[2:3] - number * PAIR_SLOTS
    pair_code = jnp.where(
        (pair_slot >= 0) & (pair_slot < PAIR_SLOTS), (position >> 1) * PAIR_SLOTS + pair_slot, -1
    )
    return position, code, pair_code


def terms_kernel(where, everything, codes, cov, out):
    row, col, number = where[0], where[1], where[2]
    rows, tile = cov.shape
    nobs = everything.shape[1]
    groups = out.shape[0]
    values = jnp.concatenate([everything[part, :, : tile // 2] for part in range(2)], axis=1)
    position, code, pair_code = slot_codes(codes, number)
    sub = iota((LANES, nobs), 0)
    pick = (code == col * SPAN + sub % SLOTS).astype(jnp.bfloat16)
    weights = halves_of(values)
    covariance = halves_of(cov[...])
    row_terms = split_dot(covariance, chosen_rows(pick, weights), ((1,), (1,)))
    parts = halves_of(row_terms)
    pair_pick = pair_code == row * PAIR_SLOTS + sub % PAIR_SLOTS
    column_terms = jnp.zeros((LANES, tile), jnp.float32)
    gram_terms = jnp.zeros((nobs, LANES), jnp.float32)
    position_column = jnp.broadcast_to(position, (LANES, nobs)).astype(jnp.float32).T[:, :1]
    for t in range(2):
        place = 2 * row + t
        lines = slice(t * tile, (t + 1) * tile)
        off_diagonal = jnp.where(place != col, 1.0, 0.0)
        chosen = (pair_pick & (position == place)).astype(jnp.float32) * off_diagonal
        column_terms += split_dot(
            chosen_rows(chosen.astype(jnp.bfloat16), weights), tuple(part[lines] for part in covariance)
        )
        inside = (position_column == place.astype(jnp.float32)).astype(jnp.float32)
        gram_terms += split_dot(
            halves_of(values * inside), tuple(part[lines] for part in parts)
        )
    lane = iota((groups, 8, LANES), 2)
    shaped = row_terms.reshape(groups, GROUPS, 8, LANES)
    first = gram_terms.reshape(groups, 8, LANES)
    for m in range(GROUPS):
        first = jnp.where(lane // SLOTS == m, shaped[:, m], first)
    out[:, :8] = first
    owners = groups // 2
    shaped = column_terms.T.reshape(owners, GROUPS, 8, LANES)
    lane = iota((owners, 8, LANES), 2)
    second = shaped[:, 0]
    for m in range(1, GROUPS):
        second = jnp.where(lane // PAIR_SLOTS == m, shaped[:, m], second)
    for side in range(2):
        out[side * owners : (side + 1) * owners, 8:] = second


def make_terms(where, everything, codes, cov, groups):
    return pl.pallas_call(
        terms_kernel,
        out_shape=jax.ShapeDtypeStruct((groups, 16, LANES), jnp.float32),
        in_specs=[pl.BlockSpec(memory_space=pltpu.SMEM), *in_vmem(3)],
        out_specs=pl.BlockSpec(memory_space=pltpu.VMEM),
        compiler_params=params(),
    )(where, everything, codes, cov)


def place_kernel(where, codes, arrived, placed, second):
    nobs = codes.shape[1]
    groups = arrived.shape[0]
    code = slot_codes(codes, where[2])[1]
    lane = iota((8, LANES), 1)
    parts = GROUPS + 1
    lines = [[] for _ in range(parts)]
    for g in range(groups // GROUPS):
        for part in range(parts):
            line = None
            for q in range(GROUPS):
                source = arrived[g * GROUPS + q, :8]
                shift = (q * SPAN - part * SLOTS) % LANES
                turned = pltpu.roll(source, shift, 1) if shift else source
                line = turned if line is None else jnp.where(lane // SPAN == q, turned, line)
            lines[part].append(line)
    former = jnp.concatenate([jnp.concatenate(line, axis=1) for line in lines], axis=0)
    spots = (iota((groups * SPAN, nobs), 0) == code).astype(jnp.bfloat16)
    result = placing_dot(former, spots)
    placed[...] = result[: 8 * GROUPS]
    gram = result[8 * GROUPS :]
    side = jnp.where(where[1] >= groups // 2, 1, 0)
    for r in range(second.shape[0]):
        second[r, 0] = arrived[2 * r + side, 8:]
        for part in range(nobs // LANES):
            second[r, 1 + part] = gram[:, part * LANES : (part + 1) * LANES]


def place_rows(where, codes, arrived, tr_size):
    nobs = codes.shape[1]
    return pl.pallas_call(
        place_kernel,
        out_shape=(
            jax.ShapeDtypeStruct((8 * GROUPS, nobs), jnp.float32),
            jax.ShapeDtypeStruct((tr_size, 1 + nobs // LANES, 8, LANES), jnp.float32),
        ),
        in_specs=[pl.BlockSpec(memory_space=pltpu.SMEM), *in_vmem(2)],
        out_specs=tuple(in_vmem(2)),
        compiler_params=params(),
    )(where, codes, arrived)


def gather_kernel(where, codes, placed, arrived, out):
    nobs = codes.shape[1]
    pair_code = slot_codes(codes, where[2])[2]
    lane = iota((8, LANES), 1)
    pairs = arrived.shape[0]
    lines = []
    for m in range(GROUPS):
        inside = lane // PAIR_SLOTS == m
        lines.append(
            jnp.concatenate([jnp.where(inside, arrived[r, 0], 0.0) for r in range(pairs)], axis=1)
        )
    former = jnp.concatenate(lines, axis=0)
    at = iota((pairs * LANES, nobs), 0)
    spot = at // LANES * PAIR_SLOTS + at % PAIR_SLOTS
    spots = (spot == pair_code).astype(jnp.bfloat16)
    out[: 8 * GROUPS] = placed[...] + placing_dot(former, spots)
    for part in range(nobs // LANES):
        total = arrived[0, 1 + part]
        for r in range(1, pairs):
            total = total + arrived[r, 1 + part]
        out[8 * GROUPS :, part * LANES : (part + 1) * LANES] = total


def gather_rows(where, codes, placed, arrived):
    nobs = codes.shape[1]
    return pl.pallas_call(
        gather_kernel,
        out_shape=jax.ShapeDtypeStruct((8 * GROUPS + 8, nobs), jnp.float32),
        in_specs=[pl.BlockSpec(memory_space=pltpu.SMEM), *in_vmem(3)],
        out_specs=pl.BlockSpec(memory_space=pltpu.VMEM),
        compiler_params=params(),
    )(where, codes, placed, arrived)


def source_of(place, away, count):
    return lax.rem(place + count - away, count)


def inverse_kernel(where, everything, codes, *refs):
    pieces, (out, grid, rest) = refs[:-3], refs[-3:]
    for away, piece in enumerate(pieces):
        lines = piece[:, 8 * GROUPS :].reshape(-1, codes.shape[1])
        start = source_of(where[3], away, len(pieces)) * lines.shape[0]
        grid[pl.ds(pl.multiple_of(start, 8), lines.shape[0])] = lines
    nobs = codes.shape[1]
    width = everything.shape[2] - LANES
    gram = grid[...]
    both = gram + gram.T
    position = codes[0:1]
    position_column = jnp.broadcast_to(position, (LANES, nobs)).astype(jnp.float32).T[:, :1].astype(jnp.int32)
    errors = everything[0, :, width + 1 : width + 2]
    unit = (iota((nobs, nobs), 0) == iota((nobs, nobs), 1)).astype(jnp.float32)
    innovation = jnp.where(position == position_column, 0.5 * both, both) + unit * errors
    low = jnp.min(errors, keepdims=True)
    sums = jnp.sum(jnp.abs(innovation), axis=1, keepdims=True)
    high = jnp.maximum(jnp.max(sums, keepdims=True), low)
    ratio = (high - low) / (high + low)
    base = 2.0 / (low + high)
    square = ratio * ratio
    scale = 2.0 / (2.0 - square)
    out[...] = (scale * base) * (2.0 * unit - base * innovation)
    cautious = jnp.max(high - 1000.0 * low) > 0.0
    parts = halves_of(innovation)

    def unsettled(carry):
        count, left, _ = carry
        return (left > SETTLED) & (count < 64)

    def step(carry):
        count, left, spread = carry
        gap = spread * spread
        grow = 2.0 / (2.0 - gap)
        shrunk = gap * 0.5 * grow
        exact = cautious | (left < 1e-3)

        @pl.when(exact)
        def _():
            rest[...] = unit - dot(innovation, out[...])

        @pl.when(jnp.logical_not(exact))
        def _():
            rest[...] = unit - split_dot(parts, halves_of(out[...]))

        @pl.when(cautious)
        def _():
            out[...] = grow * (out[...] + dot(out[...], rest[...]))

        @pl.when(jnp.logical_not(cautious))
        def _():
            out[...] = grow * (out[...] + split_dot(halves_of(out[...]), halves_of(rest[...])))

        return count + 1, jnp.max(shrunk), shrunk

    first = square * 0.5 * scale
    lax.while_loop(unsettled, step, (jnp.int32(0), jnp.max(first), first))


def invert(where, everything, codes, pieces):
    nobs = codes.shape[1]
    return pl.pallas_call(
        inverse_kernel,
        out_shape=jax.ShapeDtypeStruct((nobs, nobs), jnp.float32),
        in_specs=[pl.BlockSpec(memory_space=pltpu.SMEM), *in_vmem(2 + len(pieces))],
        out_specs=pl.BlockSpec(memory_space=pltpu.VMEM),
        scratch_shapes=[pltpu.VMEM((nobs, nobs), jnp.float32)] * 2,
        compiler_params=params(),
        cost_estimate=pl.CostEstimate(
            flops=1500 * nobs**3, bytes_accessed=8 * nobs * nobs, transcendentals=0
        ),
    )(where, everything, codes, *pieces)


def update_kernel(where, keep, cov, col_cross, inverse, *refs):
    pieces, (out, held, left) = refs[:-3], refs[-3:]
    tile = cov.shape[1]
    nobs = inverse.shape[0]
    lines = jnp.swapaxes(col_cross[...], 0, 1).reshape(tile, nobs)
    solved = split_dot(halves_of(inverse[...]), halves_of(lines), ((1,), (1,)))
    upper, lower = halves_of(solved)
    latter = jnp.concatenate([upper, upper, lower], axis=0)
    size = 2 * tile // len(pieces)
    copies = []
    for away, piece in enumerate(pieces):
        source = source_of(where[3], away, len(pieces))
        upper, lower = halves_of(piece[:, : 8 * GROUPS].reshape(size, nobs))
        change = short(jnp.concatenate([upper, lower, upper], axis=1), latter)
        part = pl.ds(pl.multiple_of(source * size, 8), size)
        kept = keep[lax.div(source * size, tile)]
        held[away] = (cov[part] - change) * kept
        copies.append(pltpu.make_async_copy(held.at[away], out.at[part], left.at[away]))
        copies[-1].start()
    for copy in copies:
        copy.wait()


def update(where, keep, cov, col_cross, inverse, pieces):
    tile = cov.shape[1]
    count = len(pieces)
    return pl.pallas_call(
        update_kernel,
        out_shape=jax.ShapeDtypeStruct(cov.shape, jnp.float32),
        in_specs=[pl.BlockSpec(memory_space=pltpu.SMEM)] * 2 + in_vmem(3 + len(pieces)),
        out_specs=pl.BlockSpec(memory_space=pl.ANY),
        scratch_shapes=[
            pltpu.VMEM((count, 2 * tile // count, tile), jnp.float32),
            pltpu.SemaphoreType.DMA((count,)),
        ],
        compiler_params=params(),
    )(where, keep, cov, col_cross, inverse, *pieces)


def body(cov, order, stations, obs_values, obs_error):
    rows, tile = cov.shape
    nobs_own = obs_values.shape[1]
    tr_size, tc_size = lax.axis_size(TR), lax.axis_size(TC)
    nobs = nobs_own * tc_size
    row = lax.axis_index(TR)
    col = lax.axis_index(TC)

    core = lax.axis_index("k").astype(jnp.int32).reshape(1)
    packed = pack(core, stations, obs_error, obs_values[0], tc_size)
    everything = lax.all_gather(exchange(packed, TC), "k").reshape(2, nobs, tile // 2 + LANES)
    codes, rounds = make_codes(everything, order)

    def place_of(number):
        place = jnp.stack([row, col, jnp.int32(number), lax.axis_index("x")])
        return place.astype(jnp.int32)

    def one_round(number):
        where = place_of(number)
        terms = exchange(make_terms(where, everything, codes, cov, tc_size), TC)
        placed, second = place_rows(where, codes, terms, tr_size)
        return gather_rows(where, codes, placed, exchange(second, TR))

    own = lax.fori_loop(1, rounds[0], lambda number, sofar: sofar + one_round(number), one_round(0))

    moves = [
        (r * tc_size + c, c % (tc_size // 2) * tc_size + 2 * r + c // (tc_size // 2))
        for r in range(tr_size)
        for c in range(tc_size)
    ]
    moved = lax.ppermute(own[: 8 * GROUPS], ALL, moves)
    y_size, x_size = lax.axis_size(Y), lax.axis_size("x")
    near_rows = exchange(jnp.broadcast_to(own[None], (y_size, *own.shape)), Y)
    moved, near_rows = lax.optimization_barrier((moved, near_rows))
    pieces = [near_rows] + [
        lax.ppermute(near_rows, "x", [(x, (x + away) % x_size) for x in range(x_size)])
        for away in range(1, x_size)
    ]
    col_cross = exchange(jnp.broadcast_to(moved[None], (tr_size // 2, *moved.shape)), "z")
    inverse = invert(place_of(0), everything, codes, pieces)
    col_cross, inverse = lax.optimization_barrier((col_cross, inverse))
    col_cross = lax.all_gather(col_cross, "k")
    places = 2 * row + jnp.arange(2, dtype=jnp.int32)
    row_order = lax.dynamic_slice_in_dim(order, 2 * row, 2)
    col_order = lax.dynamic_slice_in_dim(order, col, 1)
    keep = ((row_order > col_order) | (places == col)).astype(jnp.float32)
    return update(place_of(0), keep, cov, col_cross, inverse, pieces)


def solution(mesh):
    tr_size, tc_size = mesh.shape["tr"], mesh.shape["tc"]
    y_size = 8 if tc_size % 8 == 0 else tc_size
    split = Mesh(
        mesh.devices.reshape(tr_size // 2, 2, tc_size // y_size, y_size // 2, 2), ALL
    )
    return jax.shard_map(
        body,
        mesh=split,
        in_specs=(P(TR, TC), P(), P(None, TC), P(None, TC, None), P(None, TC)),
        out_specs=P(TR, TC),
        check_vma=False,
    )
```

```python
import jax
import jax.numpy as jnp
from jax import lax
from jax.experimental import pallas as pl
from jax.experimental.pallas import tpu as pltpu
from jax.sharding import Mesh
from jax.sharding import PartitionSpec as P

TR = ("z", "k")
TC = ("x", "yh", "yl")
Y = ("yh", "yl")
ALL = ("z", "k", "x", "yh", "yl")
LANES = 128
SPAN = 32
GROUPS = LANES // SPAN
SLOTS = 24
PAIR_SLOTS = 32
SETTLED = 1e-7

precise = lax.Precision.HIGHEST


def dot(former, latter, dims=((1,), (0,))):
    return lax.dot_general(
        former, latter, (dims, ((), ())), precision=precise, preferred_element_type=jnp.float32
    )


def halves_of(array):
    upper = array.astype(jnp.bfloat16)
    return upper, (array - upper.astype(jnp.float32)).astype(jnp.bfloat16)


def short(former, latter, dims=((1,), (0,))):
    return lax.dot_general(former, latter, (dims, ((), ())), preferred_element_type=jnp.float32)


def split_dot(former, latter, dims=((1,), (0,))):
    return short(
        jnp.concatenate([former[0], former[1], former[0]], axis=dims[0][0]),
        jnp.concatenate([latter[0], latter[0], latter[1]], axis=dims[1][0]),
        dims,
    )


def chosen_rows(pick, pair):
    return tuple(short(pick, part).astype(jnp.bfloat16) for part in pair)


def placing_dot(former, spots):
    upper = former.astype(jnp.bfloat16)
    rest = former - upper.astype(jnp.float32)
    middle = rest.astype(jnp.bfloat16)
    lower = (rest - middle.astype(jnp.float32)).astype(jnp.bfloat16)
    return short(upper, spots) + (short(middle, spots) + short(lower, spots))


def iota(shape, dim):
    return lax.broadcasted_iota(jnp.int32, shape, dim)


def exchange(array, axes):
    return lax.all_to_all(array, axes, 0, 0, tiled=True)


def in_vmem(count):
    return [pl.BlockSpec(memory_space=pltpu.VMEM)] * count


def params():
    return pltpu.CompilerParams(vmem_limit_bytes=48 * 1024 * 1024)


def as_row(column):
    return jnp.broadcast_to(column, (column.shape[0], LANES)).T[:1]


def pack_kernel(core, stations_at, errors_at, values_at, out, stations, errors, values, arrived):
    own, width = values.shape
    cells = pl.ds(pl.multiple_of(core[0] * width, LANES), width)
    copies = [
        pltpu.make_async_copy(source, held, arrived.at[number])
        for number, (source, held) in enumerate(
            ((stations_at, stations), (errors_at, errors), (values_at.at[:, cells], values))
        )
    ]
    for copy in copies:
        copy.start()
    for copy in copies:
        copy.wait()
    diagonal = iota((own, own), 0) == iota((own, own), 1)
    station = jnp.sum(jnp.where(diagonal, stations[...].astype(jnp.float32), 0.0), axis=1, keepdims=True)
    error = jnp.sum(jnp.where(diagonal, errors[...], 0.0), axis=1, keepdims=True)
    tail = jnp.where(iota((own, LANES), 1) == 0, station, error)
    for place in range(out.shape[0]):
        out[place, :, :width] = values[...]
        out[place, :, width:] = tail


def pack(core, stations, errors, values, copies):
    own, tile = values.shape
    return pl.pallas_call(
        pack_kernel,
        out_shape=jax.ShapeDtypeStruct((copies, own, tile // 2 + LANES), jnp.float32),
        in_specs=[pl.BlockSpec(memory_space=pltpu.SMEM)] + [pl.BlockSpec(memory_space=pltpu.HBM)] * 3,
        out_specs=pl.BlockSpec(memory_space=pltpu.VMEM),
        scratch_shapes=[
            pltpu.VMEM(stations.shape, jnp.int32),
            pltpu.VMEM(errors.shape, jnp.float32),
            pltpu.VMEM((own, tile // 2), jnp.float32),
            pltpu.SemaphoreType.DMA((3,)),
        ],
        compiler_params=pltpu.CompilerParams(vmem_limit_bytes=62 * 1024 * 1024),
    )(core, stations, errors, values)


def codes_kernel(everything, order_column, codes, rounds):
    nobs = everything.shape[1]
    width = everything.shape[2] - LANES
    station = everything[0, :, width : width + 1].astype(jnp.int32)
    station_row = as_row(everything[0, :, width : width + 1]).astype(jnp.int32)
    blocks = order_column.shape[0]
    position = jnp.sum(
        jnp.where(order_column[...] == station_row, iota((blocks, nobs), 0), 0), axis=0, keepdims=True
    )
    position_column = jnp.broadcast_to(position, (LANES, nobs)).astype(jnp.float32).T[:, :1].astype(jnp.int32)
    before = iota((nobs, nobs), 0) < iota((nobs, nobs), 1)
    rank = jnp.sum(((station == station_row) & before).astype(jnp.int32), axis=0, keepdims=True)
    paired = (position_column >> 1) == (position >> 1)
    pair_rank = jnp.sum((paired & before).astype(jnp.int32), axis=0, keepdims=True)
    codes[0:1] = position
    codes[1:2] = rank
    codes[2:3] = pair_rank
    codes[3:8] = jnp.zeros((5, nobs), jnp.int32)
    rounds[0] = 1 + jnp.maximum(jnp.max(rank) // SLOTS, jnp.max(pair_rank) // PAIR_SLOTS)


def make_codes(everything, order):
    return pl.pallas_call(
        codes_kernel,
        out_shape=(
            jax.ShapeDtypeStruct((8, everything.shape[1]), jnp.int32),
            jax.ShapeDtypeStruct((1,), jnp.int32),
        ),
        in_specs=in_vmem(2),
        out_specs=(pl.BlockSpec(memory_space=pltpu.VMEM), pl.BlockSpec(memory_space=pltpu.SMEM)),
        compiler_params=params(),
    )(everything, order.reshape(-1, 1))


def slot_codes(codes, number):
    position = codes[0:1]
    slot = codes[1:2] - number * SLOTS
    code = jnp.where((slot >= 0) & (slot < SLOTS), position * SPAN + slot, -1)
    pair_slot = codes[2:3] - number * PAIR_SLOTS
    pair_code = jnp.where(
        (pair_slot >= 0) & (pair_slot < PAIR_SLOTS), (position >> 1) * PAIR_SLOTS + pair_slot, -1
    )
    return position, code, pair_code


def terms_kernel(where, everything, codes, cov, out):
    row, col, number = where[0], where[1], where[2]
    rows, tile = cov.shape
    nobs = everything.shape[1]
    groups = out.shape[0]
    values = jnp.concatenate([everything[part, :, : tile // 2] for part in range(2)], axis=1)
    position, code, pair_code = slot_codes(codes, number)
    sub = iota((LANES, nobs), 0)
    pick = (code == col * SPAN + sub % SLOTS).astype(jnp.bfloat16)
    weights = halves_of(values)
    covariance = halves_of(cov[...])
    row_terms = split_dot(covariance, chosen_rows(pick, weights), ((1,), (1,)))
    parts = halves_of(row_terms)
    pair_pick = pair_code == row * PAIR_SLOTS + sub % PAIR_SLOTS
    column_terms = jnp.zeros((LANES, tile), jnp.float32)
    gram_terms = jnp.zeros((nobs, LANES), jnp.float32)
    position_column = jnp.broadcast_to(position, (LANES, nobs)).astype(jnp.float32).T[:, :1]
    for t in range(2):
        place = 2 * row + t
        lines = slice(t * tile, (t + 1) * tile)
        off_diagonal = jnp.where(place != col, 1.0, 0.0)
        chosen = (pair_pick & (position == place)).astype(jnp.float32) * off_diagonal
        column_terms += split_dot(
            chosen_rows(chosen.astype(jnp.bfloat16), weights), tuple(part[lines] for part in covariance)
        )
        inside = (position_column == place.astype(jnp.float32)).astype(jnp.float32)
        gram_terms += split_dot(
            halves_of(values * inside), tuple(part[lines] for part in parts)
        )
    lane = iota((groups, 8, LANES), 2)
    shaped = row_terms.reshape(groups, GROUPS, 8, LANES)
    first = gram_terms.reshape(groups, 8, LANES)
    for m in range(GROUPS):
        first = jnp.where(lane // SLOTS == m, shaped[:, m], first)
    out[:, :8] = first
    owners = groups // 2
    shaped = column_terms.T.reshape(owners, GROUPS, 8, LANES)
    lane = iota((owners, 8, LANES), 2)
    second = shaped[:, 0]
    for m in range(1, GROUPS):
        second = jnp.where(lane // PAIR_SLOTS == m, shaped[:, m], second)
    for side in range(2):
        out[side * owners : (side + 1) * owners, 8:] = second


def make_terms(where, everything, codes, cov, groups):
    return pl.pallas_call(
        terms_kernel,
        out_shape=jax.ShapeDtypeStruct((groups, 16, LANES), jnp.float32),
        in_specs=[pl.BlockSpec(memory_space=pltpu.SMEM), *in_vmem(3)],
        out_specs=pl.BlockSpec(memory_space=pltpu.VMEM),
        compiler_params=params(),
    )(where, everything, codes, cov)


def place_kernel(where, codes, arrived, placed, second):
    nobs = codes.shape[1]
    groups = arrived.shape[0]
    code = slot_codes(codes, where[2])[1]
    lane = iota((8, LANES), 1)
    parts = GROUPS + 1
    lines = [[] for _ in range(parts)]
    for g in range(groups // GROUPS):
        for part in range(parts):
            line = None
            for q in range(GROUPS):
                source = arrived[g * GROUPS + q, :8]
                shift = (q * SPAN - part * SLOTS) % LANES
                turned = pltpu.roll(source, shift, 1) if shift else source
                line = turned if line is None else jnp.where(lane // SPAN == q, turned, line)
            lines[part].append(line)
    former = jnp.concatenate([jnp.concatenate(line, axis=1) for line in lines], axis=0)
    spots = (iota((groups * SPAN, nobs), 0) == code).astype(jnp.bfloat16)
    result = placing_dot(former, spots)
    placed[...] = result[: 8 * GROUPS]
    gram = result[8 * GROUPS :]
    side = jnp.where(where[1] >= groups // 2, 1, 0)
    for r in range(second.shape[0]):
        second[r, 0] = arrived[2 * r + side, 8:]
        for part in range(nobs // LANES):
            second[r, 1 + part] = gram[:, part * LANES : (part + 1) * LANES]


def place_rows(where, codes, arrived, tr_size):
    nobs = codes.shape[1]
    return pl.pallas_call(
        place_kernel,
        out_shape=(
            jax.ShapeDtypeStruct((8 * GROUPS, nobs), jnp.float32),
            jax.ShapeDtypeStruct((tr_size, 1 + nobs // LANES, 8, LANES), jnp.float32),
        ),
        in_specs=[pl.BlockSpec(memory_space=pltpu.SMEM), *in_vmem(2)],
        out_specs=tuple(in_vmem(2)),
        compiler_params=params(),
    )(where, codes, arrived)


def gather_kernel(where, codes, placed, arrived, out):
    nobs = codes.shape[1]
    pair_code = slot_codes(codes, where[2])[2]
    lane = iota((8, LANES), 1)
    pairs = arrived.shape[0]
    lines = []
    for m in range(GROUPS):
        inside = lane // PAIR_SLOTS == m
        lines.append(
            jnp.concatenate([jnp.where(inside, arrived[r, 0], 0.0) for r in range(pairs)], axis=1)
        )
    former = jnp.concatenate(lines, axis=0)
    at = iota((pairs * LANES, nobs), 0)
    spot = at // LANES * PAIR_SLOTS + at % PAIR_SLOTS
    spots = (spot == pair_code).astype(jnp.bfloat16)
    out[: 8 * GROUPS] = placed[...] + placing_dot(former, spots)
    for part in range(nobs // LANES):
        total = arrived[0, 1 + part]
        for r in range(1, pairs):
            total = total + arrived[r, 1 + part]
        out[8 * GROUPS :, part * LANES : (part + 1) * LANES] = total


def gather_rows(where, codes, placed, arrived):
    nobs = codes.shape[1]
    return pl.pallas_call(
        gather_kernel,
        out_shape=jax.ShapeDtypeStruct((8 * GROUPS + 8, nobs), jnp.float32),
        in_specs=[pl.BlockSpec(memory_space=pltpu.SMEM), *in_vmem(3)],
        out_specs=pl.BlockSpec(memory_space=pltpu.VMEM),
        compiler_params=params(),
    )(where, codes, placed, arrived)


def distances(count):
    return sorted(range(count), key=lambda away: min(away, count - away))


def source_of(place, away, count):
    return lax.rem(place + count - away, count)


def inverse_kernel(where, everything, codes, *refs):
    pieces, (out, grid, rest) = refs[:-3], refs[-3:]
    for away, piece in zip(distances(len(pieces)), pieces):
        lines = piece[:, 8 * GROUPS :].reshape(-1, codes.shape[1])
        start = source_of(where[3], away, len(pieces)) * lines.shape[0]
        grid[pl.ds(pl.multiple_of(start, 8), lines.shape[0])] = lines
    nobs = codes.shape[1]
    width = everything.shape[2] - LANES
    gram = grid[...]
    both = gram + gram.T
    position = codes[0:1]
    position_column = jnp.broadcast_to(position, (LANES, nobs)).astype(jnp.float32).T[:, :1].astype(jnp.int32)
    errors = everything[0, :, width + 1 : width + 2]
    unit = (iota((nobs, nobs), 0) == iota((nobs, nobs), 1)).astype(jnp.float32)
    innovation = jnp.where(position == position_column, 0.5 * both, both) + unit * errors
    low = jnp.min(errors, keepdims=True)
    sums = jnp.sum(jnp.abs(innovation), axis=1, keepdims=True)
    high = jnp.maximum(jnp.max(sums, keepdims=True), low)
    ratio = (high - low) / (high + low)
    base = 2.0 / (low + high)
    square = ratio * ratio
    scale = 2.0 / (2.0 - square)
    out[...] = (scale * base) * (2.0 * unit - base * innovation)
    cautious = jnp.max(high - 1000.0 * low) > 0.0
    parts = halves_of(innovation)

    def unsettled(carry):
        count, left, _ = carry
        return (left > SETTLED) & (count < 64)

    def step(carry):
        count, left, spread = carry
        gap = spread * spread
        grow = 2.0 / (2.0 - gap)
        shrunk = gap * 0.5 * grow
        exact = cautious | (left < 1e-3)

        @pl.when(exact)
        def _():
            rest[...] = unit - dot(innovation, out[...])

        @pl.when(jnp.logical_not(exact))
        def _():
            rest[...] = unit - split_dot(parts, halves_of(out[...]))

        @pl.when(cautious)
        def _():
            out[...] = grow * (out[...] + dot(out[...], rest[...]))

        @pl.when(jnp.logical_not(cautious))
        def _():
            out[...] = grow * (out[...] + split_dot(halves_of(out[...]), halves_of(rest[...])))

        return count + 1, jnp.max(shrunk), shrunk

    first = square * 0.5 * scale
    lax.while_loop(unsettled, step, (jnp.int32(0), jnp.max(first), first))


def invert(where, everything, codes, pieces):
    nobs = codes.shape[1]
    return pl.pallas_call(
        inverse_kernel,
        out_shape=jax.ShapeDtypeStruct((nobs, nobs), jnp.float32),
        in_specs=[pl.BlockSpec(memory_space=pltpu.SMEM), *in_vmem(2 + len(pieces))],
        out_specs=pl.BlockSpec(memory_space=pltpu.VMEM),
        scratch_shapes=[pltpu.VMEM((nobs, nobs), jnp.float32)] * 2,
        compiler_params=params(),
        cost_estimate=pl.CostEstimate(
            flops=1500 * nobs**3, bytes_accessed=8 * nobs * nobs, transcendentals=0
        ),
    )(where, everything, codes, *pieces)


def update_kernel(where, order, cov, col_cross, inverse, *refs):
    pieces, (out, held, left) = refs[:-3], refs[-3:]
    tile = cov.shape[1]
    nobs = inverse.shape[0]
    lines = jnp.swapaxes(col_cross[...], 0, 1).reshape(tile, nobs)
    solved = split_dot(halves_of(inverse[...]), halves_of(lines), ((1,), (1,)))
    upper, lower = halves_of(solved)
    latter = jnp.concatenate([upper, upper, lower], axis=0)
    size = 2 * tile // len(pieces)
    copies = []
    for away, piece in zip(distances(len(pieces)), pieces):
        source = source_of(where[3], away, len(pieces))
        upper, lower = halves_of(piece[:, : 8 * GROUPS].reshape(size, nobs))
        change = short(jnp.concatenate([upper, lower, upper], axis=1), latter)
        part = pl.ds(pl.multiple_of(source * size, 8), size)
        place = 2 * where[0] + lax.div(source * size, tile)
        live = (order[place] > order[where[1]]) | (place == where[1])
        kept = jnp.where(live, 1.0, 0.0)
        held[away] = (cov[part] - change) * kept
        copies.append(pltpu.make_async_copy(held.at[away], out.at[part], left.at[away]))
        copies[-1].start()
    for copy in copies:
        copy.wait()


def update(where, order, cov, col_cross, inverse, pieces):
    tile = cov.shape[1]
    count = len(pieces)
    return pl.pallas_call(
        update_kernel,
        out_shape=jax.ShapeDtypeStruct(cov.shape, jnp.float32),
        in_specs=[pl.BlockSpec(memory_space=pltpu.SMEM)] * 2 + in_vmem(3 + len(pieces)),
        out_specs=pl.BlockSpec(memory_space=pl.ANY),
        scratch_shapes=[
            pltpu.VMEM((count, 2 * tile // count, tile), jnp.float32),
            pltpu.SemaphoreType.DMA((count,)),
        ],
        compiler_params=params(),
    )(where, order, cov, col_cross, inverse, *pieces)


def body(cov, order, stations, obs_values, obs_error):
    rows, tile = cov.shape
    nobs_own = obs_values.shape[1]
    tr_size, tc_size = lax.axis_size(TR), lax.axis_size(TC)
    nobs = nobs_own * tc_size
    row = lax.axis_index(TR)
    col = lax.axis_index(TC)

    core = lax.axis_index("k").astype(jnp.int32).reshape(1)
    packed = pack(core, stations, obs_error, obs_values[0], tc_size)
    everything = lax.all_gather(exchange(packed, TC), "k").reshape(2, nobs, tile // 2 + LANES)
    codes, rounds = make_codes(everything, order)

    def place_of(number):
        place = jnp.stack([row, col, jnp.int32(number), lax.axis_index("x")])
        return place.astype(jnp.int32)

    def one_round(number):
        where = place_of(number)
        terms = exchange(make_terms(where, everything, codes, cov, tc_size), TC)
        placed, second = place_rows(where, codes, terms, tr_size)
        return gather_rows(where, codes, placed, exchange(second, TR))

    own = lax.fori_loop(1, rounds[0], lambda number, sofar: sofar + one_round(number), one_round(0))

    moves = [
        (r * tc_size + c, c % (tc_size // 2) * tc_size + 2 * r + c // (tc_size // 2))
        for r in range(tr_size)
        for c in range(tc_size)
    ]
    moved = lax.ppermute(own[: 8 * GROUPS], ALL, moves)
    y_size, x_size = lax.axis_size(Y), lax.axis_size("x")
    near_rows = exchange(jnp.broadcast_to(own[None], (y_size, *own.shape)), Y)
    moved, near_rows = lax.optimization_barrier((moved, near_rows))
    pieces = [near_rows] + [
        lax.ppermute(near_rows, "x", [(x, (x + away) % x_size) for x in range(x_size)])
        for away in distances(x_size)[1:]
    ]
    col_cross = exchange(jnp.broadcast_to(moved[None], (tr_size // 2, *moved.shape)), "z")
    inverse = invert(place_of(0), everything, codes, pieces)
    col_cross, inverse = lax.optimization_barrier((col_cross, inverse))
    col_cross = lax.all_gather(col_cross, "k")
    return update(place_of(0), order, cov, col_cross, inverse, pieces)


def solution(mesh):
    tr_size, tc_size = mesh.shape["tr"], mesh.shape["tc"]
    y_size = 8 if tc_size % 8 == 0 else tc_size
    split = Mesh(
        mesh.devices.reshape(tr_size // 2, 2, tc_size // y_size, y_size // 2, 2), ALL
    )
    return jax.shard_map(
        body,
        mesh=split,
        in_specs=(P(TR, TC), P(), P(None, TC), P(None, TC, None), P(None, TC)),
        out_specs=P(TR, TC),
        check_vma=False,
    )
```

```python
import jax
import jax.numpy as jnp
from jax import lax
from jax.experimental import pallas as pl
from jax.experimental.pallas import tpu as pltpu
from jax.sharding import Mesh
from jax.sharding import PartitionSpec as P

TR = ("z", "k")
TC = ("x", "yh", "yl")
Y = ("yh", "yl")
ALL = ("z", "k", "x", "yh", "yl")
LANES = 128
SPAN = 32
GROUPS = LANES // SPAN
SLOTS = 24
PAIR_SLOTS = 32
SETTLED = 1e-7

precise = lax.Precision.HIGHEST


def dot(former, latter, dims=((1,), (0,))):
    return lax.dot_general(
        former, latter, (dims, ((), ())), precision=precise, preferred_element_type=jnp.float32
    )


def halves_of(array):
    upper = array.astype(jnp.bfloat16)
    return upper, (array - upper.astype(jnp.float32)).astype(jnp.bfloat16)


def short(former, latter, dims=((1,), (0,))):
    return lax.dot_general(former, latter, (dims, ((), ())), preferred_element_type=jnp.float32)


def split_dot(former, latter, dims=((1,), (0,))):
    return short(
        jnp.concatenate([former[0], former[1], former[0]], axis=dims[0][0]),
        jnp.concatenate([latter[0], latter[0], latter[1]], axis=dims[1][0]),
        dims,
    )


def chosen_rows(pick, pair):
    return tuple(short(pick, part).astype(jnp.bfloat16) for part in pair)


def placing_dot(former, spots):
    upper = former.astype(jnp.bfloat16)
    rest = former - upper.astype(jnp.float32)
    middle = rest.astype(jnp.bfloat16)
    lower = (rest - middle.astype(jnp.float32)).astype(jnp.bfloat16)
    return short(upper, spots) + (short(middle, spots) + short(lower, spots))


def iota(shape, dim):
    return lax.broadcasted_iota(jnp.int32, shape, dim)


def exchange(array, axes):
    return lax.all_to_all(array, axes, 0, 0, tiled=True)


def in_vmem(count):
    return [pl.BlockSpec(memory_space=pltpu.VMEM)] * count


def params():
    return pltpu.CompilerParams(vmem_limit_bytes=48 * 1024 * 1024)


def as_row(column):
    return jnp.broadcast_to(column, (column.shape[0], LANES)).T[:1]


def pack_kernel(core, stations_at, errors_at, values_at, out, stations, errors, values, arrived):
    own, width = values.shape
    cells = pl.ds(pl.multiple_of(core[0] * width, LANES), width)
    copies = [
        pltpu.make_async_copy(source, held, arrived.at[number])
        for number, (source, held) in enumerate(
            ((stations_at, stations), (errors_at, errors), (values_at.at[:, cells], values))
        )
    ]
    for copy in copies:
        copy.start()
    for copy in copies:
        copy.wait()
    diagonal = iota((own, own), 0) == iota((own, own), 1)
    station = jnp.sum(jnp.where(diagonal, stations[...].astype(jnp.float32), 0.0), axis=1, keepdims=True)
    error = jnp.sum(jnp.where(diagonal, errors[...], 0.0), axis=1, keepdims=True)
    tail = jnp.where(iota((own, LANES), 1) == 0, station, error)
    for place in range(out.shape[0]):
        out[place, :, :width] = values[...]
        out[place, :, width:] = tail


def pack(core, stations, errors, values, copies):
    own, tile = values.shape
    return pl.pallas_call(
        pack_kernel,
        out_shape=jax.ShapeDtypeStruct((copies, own, tile // 2 + LANES), jnp.float32),
        in_specs=[pl.BlockSpec(memory_space=pltpu.SMEM)] + [pl.BlockSpec(memory_space=pltpu.HBM)] * 3,
        out_specs=pl.BlockSpec(memory_space=pltpu.VMEM),
        scratch_shapes=[
            pltpu.VMEM(stations.shape, jnp.int32),
            pltpu.VMEM(errors.shape, jnp.float32),
            pltpu.VMEM((own, tile // 2), jnp.float32),
            pltpu.SemaphoreType.DMA((3,)),
        ],
        compiler_params=pltpu.CompilerParams(vmem_limit_bytes=62 * 1024 * 1024),
    )(core, stations, errors, values)


def codes_kernel(everything, order_column, codes, rounds):
    nobs = everything.shape[1]
    width = everything.shape[2] - LANES
    station = everything[0, :, width : width + 1].astype(jnp.int32)
    station_row = as_row(everything[0, :, width : width + 1]).astype(jnp.int32)
    blocks = order_column.shape[0]
    position = jnp.sum(
        jnp.where(order_column[...] == station_row, iota((blocks, nobs), 0), 0), axis=0, keepdims=True
    )
    position_column = jnp.broadcast_to(position, (LANES, nobs)).astype(jnp.float32).T[:, :1].astype(jnp.int32)
    before = iota((nobs, nobs), 0) < iota((nobs, nobs), 1)
    rank = jnp.sum(((station == station_row) & before).astype(jnp.int32), axis=0, keepdims=True)
    paired = (position_column >> 1) == (position >> 1)
    pair_rank = jnp.sum((paired & before).astype(jnp.int32), axis=0, keepdims=True)
    codes[0:1] = position
    codes[1:2] = rank
    codes[2:3] = pair_rank
    codes[3:8] = jnp.zeros((5, nobs), jnp.int32)
    rounds[0] = 1 + jnp.maximum(jnp.max(rank) // SLOTS, jnp.max(pair_rank) // PAIR_SLOTS)


def make_codes(everything, order):
    return pl.pallas_call(
        codes_kernel,
        out_shape=(
            jax.ShapeDtypeStruct((8, everything.shape[1]), jnp.int32),
            jax.ShapeDtypeStruct((1,), jnp.int32),
        ),
        in_specs=in_vmem(2),
        out_specs=(pl.BlockSpec(memory_space=pltpu.VMEM), pl.BlockSpec(memory_space=pltpu.SMEM)),
        compiler_params=params(),
    )(everything, order.reshape(-1, 1))


def slot_codes(codes, number):
    position = codes[0:1]
    slot = codes[1:2] - number * SLOTS
    code = jnp.where((slot >= 0) & (slot < SLOTS), position * SPAN + slot, -1)
    pair_slot = codes[2:3] - number * PAIR_SLOTS
    pair_code = jnp.where(
        (pair_slot >= 0) & (pair_slot < PAIR_SLOTS), (position >> 1) * PAIR_SLOTS + pair_slot, -1
    )
    return position, code, pair_code


def terms_kernel(where, everything, codes, cov, out):
    row, col, number = where[0], where[1], where[2]
    rows, tile = cov.shape
    nobs = everything.shape[1]
    groups = out.shape[0]
    values = jnp.concatenate([everything[part, :, : tile // 2] for part in range(2)], axis=1)
    position, code, pair_code = slot_codes(codes, number)
    sub = iota((LANES, nobs), 0)
    pick = (code == col * SPAN + sub % SLOTS).astype(jnp.bfloat16)
    weights = halves_of(values)
    covariance = halves_of(cov[...])
    row_terms = split_dot(covariance, chosen_rows(pick, weights), ((1,), (1,)))
    parts = halves_of(row_terms)
    pair_pick = pair_code == row * PAIR_SLOTS + sub % PAIR_SLOTS
    column_terms = jnp.zeros((LANES, tile), jnp.float32)
    gram_terms = jnp.zeros((nobs, LANES), jnp.float32)
    position_column = jnp.broadcast_to(position, (LANES, nobs)).astype(jnp.float32).T[:, :1]
    for t in range(2):
        place = 2 * row + t
        lines = slice(t * tile, (t + 1) * tile)
        off_diagonal = jnp.where(place != col, 1.0, 0.0)
        chosen = (pair_pick & (position == place)).astype(jnp.float32) * off_diagonal
        column_terms += split_dot(
            chosen_rows(chosen.astype(jnp.bfloat16), weights), tuple(part[lines] for part in covariance)
        )
        inside = (position_column == place.astype(jnp.float32)).astype(jnp.float32)
        gram_terms += split_dot(
            halves_of(values * inside), tuple(part[lines] for part in parts)
        )
    lane = iota((groups, 8, LANES), 2)
    shaped = row_terms.reshape(groups, GROUPS, 8, LANES)
    first = gram_terms.reshape(groups, 8, LANES)
    for m in range(GROUPS):
        first = jnp.where(lane // SLOTS == m, shaped[:, m], first)
    out[:, :8] = first
    owners = groups // 2
    shaped = column_terms.T.reshape(owners, GROUPS, 8, LANES)
    lane = iota((owners, 8, LANES), 2)
    second = shaped[:, 0]
    for m in range(1, GROUPS):
        second = jnp.where(lane // PAIR_SLOTS == m, shaped[:, m], second)
    for side in range(2):
        out[side * owners : (side + 1) * owners, 8:] = second


def make_terms(where, everything, codes, cov, groups):
    return pl.pallas_call(
        terms_kernel,
        out_shape=jax.ShapeDtypeStruct((groups, 16, LANES), jnp.float32),
        in_specs=[pl.BlockSpec(memory_space=pltpu.SMEM), *in_vmem(3)],
        out_specs=pl.BlockSpec(memory_space=pltpu.VMEM),
        compiler_params=params(),
    )(where, everything, codes, cov)


def place_kernel(where, codes, arrived, placed, second):
    nobs = codes.shape[1]
    groups = arrived.shape[0]
    code = slot_codes(codes, where[2])[1]
    lane = iota((8, LANES), 1)
    parts = GROUPS + 1
    lines = [[] for _ in range(parts)]
    for g in range(groups // GROUPS):
        for part in range(parts):
            line = None
            for q in range(GROUPS):
                source = arrived[g * GROUPS + q, :8]
                shift = (q * SPAN - part * SLOTS) % LANES
                turned = pltpu.roll(source, shift, 1) if shift else source
                line = turned if line is None else jnp.where(lane // SPAN == q, turned, line)
            lines[part].append(line)
    former = jnp.concatenate([jnp.concatenate(line, axis=1) for line in lines], axis=0)
    spots = (iota((groups * SPAN, nobs), 0) == code).astype(jnp.bfloat16)
    result = placing_dot(former, spots)
    placed[...] = result[: 8 * GROUPS]
    gram = result[8 * GROUPS :]
    side = jnp.where(where[1] >= groups // 2, 1, 0)
    for r in range(second.shape[0]):
        second[r, 0] = arrived[2 * r + side, 8:]
        for part in range(nobs // LANES):
            second[r, 1 + part] = gram[:, part * LANES : (part + 1) * LANES]


def place_rows(where, codes, arrived, tr_size):
    nobs = codes.shape[1]
    return pl.pallas_call(
        place_kernel,
        out_shape=(
            jax.ShapeDtypeStruct((8 * GROUPS, nobs), jnp.float32),
            jax.ShapeDtypeStruct((tr_size, 1 + nobs // LANES, 8, LANES), jnp.float32),
        ),
        in_specs=[pl.BlockSpec(memory_space=pltpu.SMEM), *in_vmem(2)],
        out_specs=tuple(in_vmem(2)),
        compiler_params=params(),
    )(where, codes, arrived)


def gather_kernel(where, codes, placed, arrived, out):
    nobs = codes.shape[1]
    pair_code = slot_codes(codes, where[2])[2]
    lane = iota((8, LANES), 1)
    pairs = arrived.shape[0]
    lines = []
    for m in range(GROUPS):
        inside = lane // PAIR_SLOTS == m
        lines.append(
            jnp.concatenate([jnp.where(inside, arrived[r, 0], 0.0) for r in range(pairs)], axis=1)
        )
    former = jnp.concatenate(lines, axis=0)
    at = iota((pairs * LANES, nobs), 0)
    spot = at // LANES * PAIR_SLOTS + at % PAIR_SLOTS
    spots = (spot == pair_code).astype(jnp.bfloat16)
    rows = placed[...] + placing_dot(former, spots)
    for copy in range(out.shape[0]):
        out[copy, : 8 * GROUPS] = rows
    for part in range(nobs // LANES):
        total = arrived[0, 1 + part]
        for r in range(1, pairs):
            total = total + arrived[r, 1 + part]
        for copy in range(out.shape[0]):
            out[copy, 8 * GROUPS :, part * LANES : (part + 1) * LANES] = total


def gather_rows(where, codes, placed, arrived, copies):
    nobs = codes.shape[1]
    return pl.pallas_call(
        gather_kernel,
        out_shape=jax.ShapeDtypeStruct((copies, 8 * GROUPS + 8, nobs), jnp.float32),
        in_specs=[pl.BlockSpec(memory_space=pltpu.SMEM), *in_vmem(3)],
        out_specs=pl.BlockSpec(memory_space=pltpu.VMEM),
        compiler_params=params(),
    )(where, codes, placed, arrived)


def distances(count):
    return sorted(range(count), key=lambda away: min(away, count - away))


def source_of(place, away, count):
    return lax.rem(place + count - away, count)


def inverse_kernel(where, everything, codes, *refs):
    pieces, (out, grid, rest) = refs[:-3], refs[-3:]
    for away, piece in zip(distances(len(pieces)), pieces):
        lines = piece[:, 8 * GROUPS :].reshape(-1, codes.shape[1])
        start = source_of(where[3], away, len(pieces)) * lines.shape[0]
        grid[pl.ds(pl.multiple_of(start, 8), lines.shape[0])] = lines
    nobs = codes.shape[1]
    width = everything.shape[2] - LANES
    gram = grid[...]
    both = gram + gram.T
    position = codes[0:1]
    position_column = jnp.broadcast_to(position, (LANES, nobs)).astype(jnp.float32).T[:, :1].astype(jnp.int32)
    errors = everything[0, :, width + 1 : width + 2]
    unit = (iota((nobs, nobs), 0) == iota((nobs, nobs), 1)).astype(jnp.float32)
    innovation = jnp.where(position == position_column, 0.5 * both, both) + unit * errors
    low = jnp.min(errors, keepdims=True)
    sums = jnp.sum(jnp.abs(innovation), axis=1, keepdims=True)
    high = jnp.maximum(jnp.max(sums, keepdims=True), low)
    ratio = (high - low) / (high + low)
    base = 2.0 / (low + high)
    square = ratio * ratio
    scale = 2.0 / (2.0 - square)
    out[...] = (scale * base) * (2.0 * unit - base * innovation)
    cautious = jnp.max(high - 1000.0 * low) > 0.0
    parts = halves_of(innovation)

    def unsettled(carry):
        count, left, _ = carry
        return (left > SETTLED) & (count < 64)

    def step(carry):
        count, left, spread = carry
        gap = spread * spread
        grow = 2.0 / (2.0 - gap)
        shrunk = gap * 0.5 * grow
        exact = cautious | (left < 1e-3)

        @pl.when(exact)
        def _():
            rest[...] = unit - dot(innovation, out[...])

        @pl.when(jnp.logical_not(exact))
        def _():
            rest[...] = unit - split_dot(parts, halves_of(out[...]))

        @pl.when(cautious)
        def _():
            out[...] = grow * (out[...] + dot(out[...], rest[...]))

        @pl.when(jnp.logical_not(cautious))
        def _():
            out[...] = grow * (out[...] + split_dot(halves_of(out[...]), halves_of(rest[...])))

        return count + 1, jnp.max(shrunk), shrunk

    first = square * 0.5 * scale
    lax.while_loop(unsettled, step, (jnp.int32(0), jnp.max(first), first))


def invert(where, everything, codes, pieces):
    nobs = codes.shape[1]
    return pl.pallas_call(
        inverse_kernel,
        out_shape=jax.ShapeDtypeStruct((nobs, nobs), jnp.float32),
        in_specs=[pl.BlockSpec(memory_space=pltpu.SMEM), *in_vmem(2 + len(pieces))],
        out_specs=pl.BlockSpec(memory_space=pltpu.VMEM),
        scratch_shapes=[pltpu.VMEM((nobs, nobs), jnp.float32)] * 2,
        compiler_params=params(),
        cost_estimate=pl.CostEstimate(
            flops=1500 * nobs**3, bytes_accessed=8 * nobs * nobs, transcendentals=0
        ),
    )(where, everything, codes, *pieces)


def update_kernel(where, order, cov, col_cross, inverse, *refs):
    pieces, (out, held, left) = refs[:-3], refs[-3:]
    tile = cov.shape[1]
    nobs = inverse.shape[0]
    lines = jnp.swapaxes(col_cross[...], 0, 1).reshape(tile, nobs)
    solved = split_dot(halves_of(inverse[...]), halves_of(lines), ((1,), (1,)))
    upper, lower = halves_of(solved)
    latter = jnp.concatenate([upper, upper, lower], axis=0)
    size = 2 * tile // len(pieces)
    copies = []
    for away, piece in zip(distances(len(pieces)), pieces):
        source = source_of(where[3], away, len(pieces))
        upper, lower = halves_of(piece[:, : 8 * GROUPS].reshape(size, nobs))
        change = short(jnp.concatenate([upper, lower, upper], axis=1), latter)
        part = pl.ds(pl.multiple_of(source * size, 8), size)
        place = 2 * where[0] + lax.div(source * size, tile)
        live = (order[place] > order[where[1]]) | (place == where[1])
        kept = jnp.where(live, 1.0, 0.0)
        held[away] = (cov[part] - change) * kept
        copies.append(pltpu.make_async_copy(held.at[away], out.at[part], left.at[away]))
        copies[-1].start()
    for copy in copies:
        copy.wait()


def update(where, order, cov, col_cross, inverse, pieces):
    tile = cov.shape[1]
    count = len(pieces)
    return pl.pallas_call(
        update_kernel,
        out_shape=jax.ShapeDtypeStruct(cov.shape, jnp.float32),
        in_specs=[pl.BlockSpec(memory_space=pltpu.SMEM)] * 2 + in_vmem(3 + len(pieces)),
        out_specs=pl.BlockSpec(memory_space=pl.ANY),
        scratch_shapes=[
            pltpu.VMEM((count, 2 * tile // count, tile), jnp.float32),
            pltpu.SemaphoreType.DMA((count,)),
        ],
        compiler_params=params(),
    )(where, order, cov, col_cross, inverse, *pieces)


def body(cov, order, stations, obs_values, obs_error):
    rows, tile = cov.shape
    nobs_own = obs_values.shape[1]
    tr_size, tc_size = lax.axis_size(TR), lax.axis_size(TC)
    nobs = nobs_own * tc_size
    y_size, x_size = lax.axis_size(Y), lax.axis_size("x")
    row = lax.axis_index(TR)
    col = lax.axis_index(TC)

    core = lax.axis_index("k").astype(jnp.int32).reshape(1)
    packed = pack(core, stations, obs_error, obs_values[0], tc_size)
    everything = lax.all_gather(exchange(packed, TC), "k").reshape(2, nobs, tile // 2 + LANES)
    codes, rounds = make_codes(everything, order)

    def place_of(number):
        place = jnp.stack([row, col, jnp.int32(number), lax.axis_index("x")])
        return place.astype(jnp.int32)

    def one_round(number):
        where = place_of(number)
        terms = exchange(make_terms(where, everything, codes, cov, tc_size), TC)
        placed, second = place_rows(where, codes, terms, tr_size)
        return gather_rows(where, codes, placed, exchange(second, TR), y_size)

    own = lax.fori_loop(1, rounds[0], lambda number, sofar: sofar + one_round(number), one_round(0))

    moves = [
        (r * tc_size + c, c % (tc_size // 2) * tc_size + 2 * r + c // (tc_size // 2))
        for r in range(tr_size)
        for c in range(tc_size)
    ]
    moved = lax.ppermute(own[0, : 8 * GROUPS], ALL, moves)
    near_rows = exchange(own, Y)
    moved, near_rows = lax.optimization_barrier((moved, near_rows))
    pieces = [near_rows] + [
        lax.ppermute(near_rows, "x", [(x, (x + away) % x_size) for x in range(x_size)])
        for away in distances(x_size)[1:]
    ]
    col_cross = exchange(jnp.broadcast_to(moved[None], (tr_size // 2, *moved.shape)), "z")
    inverse = invert(place_of(0), everything, codes, pieces)
    col_cross, inverse = lax.optimization_barrier((col_cross, inverse))
    col_cross = lax.all_gather(col_cross, "k")
    return update(place_of(0), order, cov, col_cross, inverse, pieces)


def solution(mesh):
    tr_size, tc_size = mesh.shape["tr"], mesh.shape["tc"]
    y_size = 8 if tc_size % 8 == 0 else tc_size
    split = Mesh(
        mesh.devices.reshape(tr_size // 2, 2, tc_size // y_size, y_size // 2, 2), ALL
    )
    return jax.shard_map(
        body,
        mesh=split,
        in_specs=(P(TR, TC), P(), P(None, TC), P(None, TC, None), P(None, TC)),
        out_specs=P(TR, TC),
        check_vma=False,
    )
```
